128 devices in a mesh: group: 2 (over core), dev: 64 (over y, z, x).
Axes of the slice: x: 4, y: 4, z: 4, core: 2. Of those that a mesh axis runs over, the one named last changes fastest.
Arguments:
- points: float32 [2048, 3, 256], P(('group', 'dev')), may hold values from -6 to 6
- charges: float32 [2048, 32, 256], P(('group', 'dev')), may hold values from -1.5 to 1.5
- basis: float32 [2048, 64, 256], P(('group', 'dev')), may hold values from -0.375 to 0.375
- leaf_transfer: float32 [2048, 64, 64], P(('group', 'dev')), may hold values from -0.1875 to 0.1875
- dev_skeleton: float32 [128, 3, 64], P(('group', 'dev')), may hold values from -6 to 6
- dev_transfer: float32 [128, 64, 64], P(('group', 'dev')), may hold values from -0.25 to 0.25
- group_skeleton: float32 [2, 3, 64], replicated, may hold values from -6 to 6
- neighbours: int32 [2048, 12], P(('group', 'dev')), may hold values from 0 to 2047, as said below
- counts: int32 [2048], P(('group', 'dev')), may hold values from 1 to 12, as said below
- far_list: int32 [128, 16], P(('group', 'dev')), may hold values from 0 to 127, as said below
Outputs:
- kernel_product: float32 [2048, 32, 256], P(('group', 'dev'))
- slope_product: float32 [2048, 32, 256], P(('group', 'dev'))
The draws below stay inside these ranges and needn't reach their ends.
Inputs may be any that keep to these rules, and one draw needn't show every extreme that they name: `neighbours`: row l starts with l itself; its other entries lie within 14 leaves of l and may repeat. `counts`: some leaf uses all 12 slots and some only one. `far_list`: entries of a row are distinct and never the row's own node.
All inputs are finite; a program needn't handle non-finite values.
Results may differ from the reference program's by a relative error of at most 0.0003.
Values sent between devices are 32-bit elements; how exact they have to be, the bound alone decides.
No kernel may reach another device: no remote copies, remote signals or barrier semaphores. Data moves between devices by JAX's collectives and lax.ppermute only.
A program may use at most 64 MiB of HBM per device.

```python
import math
import jax
import jax.numpy as jnp
from jax import lax

LEAF = 256
R = 64
NV = 32
NNB = 12
REACH = 14
FL = 16
LD = 16
NLEAF = 2048
N_GROUP = 2
DEVICES = 128


def draw_neighbours(key, part):
    key = jax.random.fold_in(key, 11)
    span = 2 * REACH
    scores = jax.random.randint(key, (NLEAF, span), 0, 1 << 20) * span + jnp.arange(span)[None, :]
    order = jnp.argsort(scores, axis=1)[:, :NNB - 1]
    offset = jnp.where(order < REACH, order - REACH, order - REACH + 1)
    leaf_ids = jnp.arange(NLEAF)[:, None]
    target = leaf_ids + offset
    target = jnp.where((target < 0) | (target >= NLEAF), leaf_ids - offset, target)
    return jnp.concatenate([leaf_ids, target], axis=1).astype(jnp.int32)


def draw_counts(key, part):
    key = jax.random.fold_in(key, 23)
    first, second = jax.random.split(key)
    lowest = jax.random.randint(first, (NLEAF // LD, 1), 1, NNB + 1)
    raw_draw = jax.random.randint(second, (NLEAF // LD, LD), 0, 1 << 20)
    result = (lowest + raw_draw % (NNB + 1 - lowest)).reshape(NLEAF)
    result = result.at[0].set(NNB).at[1].set(1)
    return result.astype(jnp.int32)


def draw_far_list(key, part):
    key = jax.random.fold_in(key, 37)
    scores = jax.random.randint(key, (DEVICES, DEVICES), 0, 1 << 20) * DEVICES + jnp.arange(DEVICES)[None, :]
    scores = scores + jnp.eye(DEVICES, dtype=jnp.int32) * (1 << 30)
    return jnp.argsort(scores, axis=1)[:, :FL].astype(jnp.int32)


def block_scale(own_key, shape, shards, least, largest):
    def one(dim, blocks):
        draws = jax.random.uniform(jax.random.fold_in(jax.random.fold_in(own_key, 6), dim), (blocks,), jnp.float32, least / len(shards), largest / len(shards))
        return jnp.repeat(jnp.exp(draws), shape[dim] // blocks).reshape((-1,) + (1,) * (len(shape) - dim - 1))

    level = one(*shards[0])
    for cut in shards[1:]:
        level = level * one(*cut)
    return level


def gaussian(stream_key, dims, deviation, limit, pieces=(), kind=jnp.bfloat16):
    level = block_scale(stream_key, dims, pieces, -0.22, 0.18) if pieces else 1.0
    entries = jax.random.normal(stream_key, dims, jnp.float32) * deviation * level
    return jnp.minimum(jnp.maximum(entries, -limit), limit).astype(kind)


def setup_inputs(seed: int = 0) -> dict:
    streams_of = jax.random.split(jax.random.key(seed), 11)
    return {
        "points": gaussian(streams_of[0], (NLEAF, 3, LEAF), 1.0, 6.0, ((0, 128),), jnp.float32),
        "charges": gaussian(streams_of[1], (NLEAF, NV, LEAF), 0.25, 1.5, ((0, 128),), jnp.float32),
        "basis": gaussian(streams_of[2], (NLEAF, R, LEAF), LEAF ** -0.5, 0.375, ((0, 128),), jnp.float32),
        "leaf_transfer": gaussian(streams_of[3], (NLEAF, R, R), (R * LD) ** -0.5, 0.1875, ((0, 128),), jnp.float32),
        "dev_skeleton": gaussian(streams_of[4], (DEVICES, 3, R), 1.0, 6.0, ((0, 128),), jnp.float32),
        "dev_transfer": gaussian(streams_of[5], (DEVICES, R, R), (R * 8) ** -0.5, 0.25, ((0, 128),), jnp.float32),
        "group_skeleton": gaussian(streams_of[6], (N_GROUP, 3, R), 1.0, 6.0, (), jnp.float32),
        "neighbours": draw_neighbours(jax.random.fold_in(streams_of[10], 71), 0),
        "counts": draw_counts(jax.random.fold_in(streams_of[10], 71), 0),
        "far_list": draw_far_list(jax.random.fold_in(streams_of[10], 71), 0),
    }


SQRT_THREE = math.sqrt(3.0)
LENGTH_SCALE = 0.8
NUGGET = 0.01
HIGH = lax.Precision.HIGHEST

def matern_pair(target, source):
    squared = jnp.float32(0.0)
    for coord in range(3):
        differ = target[..., coord, :, None] - source[..., coord, None, :]
        squared = squared + differ * differ
    scaled = SQRT_THREE / LENGTH_SCALE * jnp.sqrt(squared + NUGGET)
    decay = jnp.exp(-scaled)
    return ((1.0 + scaled) * decay, scaled * scaled * decay / LENGTH_SCALE)

def reference(points, charges, basis, leaf_transfer, dev_skeleton, dev_transfer, group_skeleton, neighbours, counts, far_list):
    coef_leaf = jnp.einsum('lvp,lap->lva', charges, basis, precision=HIGH)
    coef_dev = jnp.einsum('dlab,dlvb->dva', leaf_transfer.reshape(DEVICES, LD, R, R), coef_leaf.reshape(DEVICES, LD, NV, R), precision=HIGH)
    images = jnp.einsum('dab,dvb->dva', dev_transfer, coef_dev, precision=HIGH)
    coef_group = images.reshape(N_GROUP, DEVICES // N_GROUP, NV, R).sum(axis=1)

    def node_far(item):
        skeleton, listed = item
        kernel_value, kernel_slope = matern_pair(skeleton[None], dev_skeleton[listed])
        remote = coef_dev[listed]
        return (jnp.einsum('sab,svb->va', kernel_value, remote, precision=HIGH), jnp.einsum('sab,svb->va', kernel_slope, remote, precision=HIGH))
    far_dev, far_dev_slope = lax.map(node_far, (dev_skeleton, far_list))
    group_value, group_slope = matern_pair(group_skeleton, group_skeleton[::-1])
    other = coef_group[::-1]
    far_group = jnp.einsum('gab,gvb->gva', group_value, other, precision=HIGH)
    far_group_slope = jnp.einsum('gab,gvb->gva', group_slope, other, precision=HIGH)

    def downward(far_node, far_top):
        spread = jnp.broadcast_to(far_top[:, None], (N_GROUP, DEVICES // N_GROUP, NV, R)).reshape(DEVICES, NV, R)
        local_dev = far_node + jnp.einsum('dab,dva->dvb', dev_transfer, spread, precision=HIGH)
        per_leaf = jnp.broadcast_to(local_dev[:, None], (DEVICES, LD, NV, R)).reshape(NLEAF, NV, R)
        local_leaf = jnp.einsum('lab,lva->lvb', leaf_transfer, per_leaf, precision=HIGH)
        return jnp.einsum('lva,lap->lvp', local_leaf, basis, precision=HIGH)
    far_part = downward(far_dev, far_group)
    far_part_slope = downward(far_dev_slope, far_group_slope)

    def leaf_near(item):
        target, listed, count = item
        kernel_value, kernel_slope = matern_pair(target[None], points[listed])
        live = (jnp.arange(NNB) < count).astype(jnp.float32)[:, None, None]
        sources = charges[listed]
        return (jnp.einsum('jpq,jvq->vp', kernel_value * live, sources, precision=HIGH), jnp.einsum('jpq,jvq->vp', kernel_slope * live, sources, precision=HIGH))
    near_part, near_part_slope = lax.map(leaf_near, (points, neighbours, counts))
    return (near_part + far_part, near_part_slope + far_part_slope)
```

```python
import math

import jax
import jax.numpy as jnp
from jax import lax
from jax.experimental import pallas as pl
from jax.experimental.pallas import tpu as pltpu
from jax.sharding import PartitionSpec as P

BF = jnp.bfloat16
F32 = jnp.float32
HIGH = lax.Precision.HIGHEST
REACH = 14
NUGGET = 0.01
LENGTH = 0.8
LOG2E = math.log2(math.e)
LN2 = math.log(2.0)
ALPHA = math.sqrt(3.0) / LENGTH * LOG2E
X0 = ALPHA * ALPHA * NUGGET
VALUE_SCALE = LN2
SLOPE_SCALE = LN2 * LN2 / LENGTH
NODE_ROWS = 24
MIB = 2**20
AXES = ("group", "dev")


def dot(a, b):
    return jnp.dot(a, b, preferred_element_type=F32)


def dot32(a, b):
    return jnp.dot(a, b, preferred_element_type=F32, precision=HIGH)


def split2(x):
    hi = x.astype(BF)
    return hi, (x - hi.astype(F32)).astype(BF)


def split3(x):
    one = x.astype(BF).astype(F32)
    rest = x - one
    two = rest.astype(BF).astype(F32)
    return one, two, rest - two


def matern_terms(x):
    t = x * lax.rsqrt(x)
    e = jnp.exp2(-t)
    return (t + LOG2E) * e, x * e


def source_rows(points):
    b = points * (-2.0 * ALPHA)
    b1, b2, b3 = split3(b)
    m1, m2, m3 = split3(jnp.sum(b * b, axis=0, keepdims=True) * 0.25)
    one = jnp.ones((3, b.shape[1]), F32)
    zero = jnp.zeros((2, b.shape[1]), F32)
    return jnp.concatenate([b1, b2, b1, b2, b3, b1, b3, b2, one, m1, m2, m3, zero], axis=0)


def target_rows(points):
    a = points * ALPHA
    a1, a2, a3 = split3(a)
    n1, n2, n3 = split3(jnp.sum(a * a, axis=0, keepdims=True) + X0)
    one = jnp.ones((3, a.shape[1]), F32)
    zero = jnp.zeros((2, a.shape[1]), F32)
    return jnp.concatenate([a1, a1, a2, a2, a1, a3, a2, a3, n1, n2, n3, one, zero], axis=0)


def coef_kernel(charges, basis, leaf_transfer, dev_transfer, skeleton, out):
    leaves = charges.shape[0]
    total = jnp.zeros((32, 64), F32)
    for l in range(leaves):
        leaf = lax.dot_general(
            charges[l], basis[l], (((1,), (1,)), ((), ())), precision=HIGH, preferred_element_type=F32
        )
        total += lax.dot_general(
            leaf, leaf_transfer[l], (((1,), (1,)), ((), ())), precision=HIGH, preferred_element_type=F32
        )
    image = lax.dot_general(
        total, dev_transfer[...], (((1,), (1,)), ((), ())), precision=HIGH, preferred_element_type=F32
    )
    out[0:16, :] = jnp.concatenate([total[:16], total[16:]], axis=1)
    out[16:24, :] = jnp.zeros((8, 128), F32)
    out[16:19, 0:64] = skeleton[...]
    out[24:40, :] = jnp.concatenate([image[:16], image[16:]], axis=1)


def near_kernel(place, neighbours, counts, own, before, after, acc, wa, c2, ua, order, *slots):
    leaves, width = neighbours.shape
    pairs = leaves * width
    half = before.shape[0]
    total = leaves + 2 * half
    first = place[0] * leaves - half
    depth = len(slots) // 2
    xs, tiles = slots[:depth], slots[depth:]

    def note(i, carry):
        leaf, slot = i // width, i % width
        chosen = jnp.clip(neighbours[leaf, slot] - first, 0, total - 1)
        order[i] = jnp.where(slot < counts[leaf], chosen, total)
        return carry

    lax.fori_loop(0, pairs, note, 0)

    def prepare(ref, offset, count):
        def step(l, carry):
            rows = ref[l]
            wa[offset + l] = jnp.transpose(source_rows(rows[0:3])).astype(BF)
            hi, lo = split2(rows[8:40])
            c2[offset + l, 0:32, :] = hi
            c2[offset + l, 32:64, :] = lo
            return carry

        lax.fori_loop(0, count, step, 0)

    prepare(before, 0, half)
    prepare(own, half, leaves)
    prepare(after, half + leaves, half)
    wa[total] = wa[half]
    c2[total] = jnp.zeros(c2.shape[1:], BF)

    def aim(l, carry):
        ua[l] = target_rows(own[l, 0:3, :]).astype(BF)
        return carry

    lax.fori_loop(0, leaves, aim, 0)
    acc[...] = jnp.zeros_like(acc)
    tiles[depth - 1][...] = jnp.zeros(tiles[0].shape, BF)
    xs[0][...] = dot(wa[order[0]], ua[0])

    def gather_up(i, tile):
        c = c2[order[i]]
        target = i // width
        one, two = dot(c, tile[0]), dot(c[:32], tile[1])
        three, four = dot(c, tile[2]), dot(c[:32], tile[3])
        acc[target, 0:32, :] += one[:32] + two
        acc[target, 32:64, :] += one[32:]
        acc[target, 64:96, :] += three[:32] + four
        acc[target, 96:128, :] += three[32:]

    def step(i, b):
        after_, before_ = jnp.minimum(i + 1, pairs - 1), jnp.maximum(i - 1, 0)
        xs[(b + 1) % depth][...] = dot(wa[order[after_]], ua[after_ // width])
        value, slope = matern_terms(xs[b][...])
        tiles[b][0], tiles[b][1] = split2(value)
        tiles[b][2], tiles[b][3] = split2(slope)
        gather_up(before_, tiles[(b - 1) % depth])

    def body(j, carry):
        for u in range(depth):
            step(j * depth + u, u)
        return carry

    lax.fori_loop(0, pairs // depth, body, 0)
    gather_up(pairs - 1, tiles[depth - 1])


def far_kernel(place, far_list, mine, theirs, own_skeleton, groups, dev_transfer, leaf_transfer, basis, near,
               value_out, slope_out, coefs, kernels):
    leaves = basis.shape[0]
    rank = place[0]
    group, node = rank // 64, rank % 64
    x0, z0, y0 = node % 4, (node // 4) % 4, node // 16

    def pair_kernel(column, row):
        x = jnp.full((64, 64), X0, F32)
        for c in range(3):
            d = (column[:, c : c + 1] - row[c : c + 1, :]) * ALPHA
            x = x + d * d
        value, slope = matern_terms(x)
        return jnp.concatenate([value * VALUE_SCALE, slope * SLOPE_SCALE], axis=1)

    own = own_skeleton[...]
    for j in range(far_list.shape[1]):
        s = far_list[0, j]
        d = s % 64
        jx, jz, jy = (x0 - d % 4 + 4) % 4, (z0 - (d // 4) % 4 + 4) % 4, (y0 - d // 16 + 4) % 4
        row = pl.multiple_of(((jy * 4 + jz) * 4 + jx) * NODE_ROWS, 8)
        block = jnp.where(s // 64 == group, mine[pl.ds(row, NODE_ROWS), :], theirs[pl.ds(row, NODE_ROWS), :])
        coefs[:, 64 * j : 64 * j + 64] = jnp.concatenate([block[:16, :64], block[:16, 64:]], axis=0)
        kernels[64 * j : 64 * j + 64, :] = pair_kernel(jnp.transpose(block[16:24, :])[:64], own)
    far = dot32(coefs[...], kernels[...])
    other = theirs[theirs.shape[0] - 16 :, :]
    other = jnp.concatenate([other[:, :64], other[:, 64:]], axis=0)
    near_group, far_group = groups[:, pl.ds(group, 1), :][:, 0], groups[:, pl.ds(1 - group, 1), :][:, 0]
    column = jnp.transpose(jnp.concatenate([far_group, jnp.zeros((5, 64), F32)], axis=0))
    top = dot32(other, pair_kernel(column, near_group))
    far = jnp.concatenate([far[:, :64], far[:, 64:]], axis=0)
    top = jnp.concatenate([top[:, :64], top[:, 64:]], axis=0)
    local_dev = far + dot32(top, dev_transfer[...])
    for l in range(leaves):
        part = dot32(dot32(local_dev, leaf_transfer[l]), basis[l])
        value_out[l] = (near[l, 0:32, :] + near[l, 32:64, :]) * VALUE_SCALE + part[:32]
        slope_out[l] = (near[l, 64:96, :] + near[l, 96:128, :]) * SLOPE_SCALE + part[32:]


VMEM = pl.BlockSpec(memory_space=pltpu.VMEM)
SMEM = pl.BlockSpec(memory_space=pltpu.SMEM)


def dev_shift(div, step):
    return [(i, i - (i // div) % 4 * div + ((i // div) % 4 + step) % 4 * div) for i in range(64)]


def gather_nodes(block):
    for div in (1, 4, 16):
        came = [block] + [lax.ppermute(block, "dev", dev_shift(div, k)) for k in (1, 2, 3)]
        images = (came[0][-16:] + came[1][-16:]) + (came[2][-16:] + came[3][-16:])
        block = jnp.concatenate([c[:-16] for c in came] + [images], axis=0)
    return block


def local(points, charges, basis, leaf_transfer, dev_skeleton, dev_transfer, group_skeleton, neighbours, counts, far_list):
    leaves = points.shape[0]
    rank = lax.axis_index(AXES)
    place = jnp.full((1,), rank, jnp.int32)
    stacked = jnp.concatenate([points, jnp.zeros((leaves, 5, 256), F32), charges], axis=1)
    size = lax.axis_size(AXES)
    up = [(i, i + 1) for i in range(size - 1)]
    down = [(j, i) for i, j in up]
    before = lax.ppermute(stacked[leaves - REACH :], AXES, up)
    after = lax.ppermute(stacked[:REACH], AXES, down)
    block = pl.pallas_call(
        coef_kernel,
        out_shape=jax.ShapeDtypeStruct((40, 128), F32),
        in_specs=[VMEM] * 5,
        out_specs=VMEM,
        compiler_params=pltpu.CompilerParams(vmem_limit_bytes=32 * MIB),
    )(charges, basis, leaf_transfer, dev_transfer[0], dev_skeleton[0])
    mine = gather_nodes(block)
    theirs = lax.ppermute(mine, "group", [(0, 1), (1, 0)])
    total = leaves + 2 * REACH
    depth = 4
    near = pl.pallas_call(
        near_kernel,
        out_shape=jax.ShapeDtypeStruct((leaves, 128, 256), F32),
        in_specs=[SMEM] * 3 + [VMEM] * 3,
        out_specs=VMEM,
        scratch_shapes=[
            pltpu.VMEM((total + 1, 256, 32), BF),
            pltpu.VMEM((total + 1, 64, 256), BF),
            pltpu.VMEM((leaves, 32, 256), BF),
            pltpu.SMEM((leaves * neighbours.shape[1],), jnp.int32),
        ]
        + [pltpu.VMEM((256, 256), F32)] * depth
        + [pltpu.VMEM((4, 256, 256), BF)] * depth,
        compiler_params=pltpu.CompilerParams(vmem_limit_bytes=40 * MIB),
    )(place, neighbours, counts, stacked, before, after)
    out = jax.ShapeDtypeStruct((leaves, 32, 256), F32)
    return pl.pallas_call(
        far_kernel,
        out_shape=(out, out),
        in_specs=[SMEM] * 2 + [VMEM] * 8,
        out_specs=(VMEM, VMEM),
        scratch_shapes=[pltpu.VMEM((32, 1024), F32), pltpu.VMEM((1024, 128), F32)],
        compiler_params=pltpu.CompilerParams(vmem_limit_bytes=32 * MIB),
    )(place, far_list, mine, theirs, dev_skeleton[0], jnp.transpose(group_skeleton, (1, 0, 2)), dev_transfer[0],
      leaf_transfer, basis, near)


def solution(mesh):
    leaf = P(AXES, None, None)
    placed = (leaf, leaf, leaf, leaf, leaf, leaf, P(), P(AXES, None), P(AXES), P(AXES, None))
    return jax.shard_map(local, mesh=mesh, in_specs=placed, out_specs=(leaf, leaf), check_vma=False)
```

```python
import math

import jax
import jax.numpy as jnp
from jax import lax
from jax.experimental import pallas as pl
from jax.experimental.pallas import tpu as pltpu
from jax.sharding import PartitionSpec as P

BF = jnp.bfloat16
F32 = jnp.float32
HIGH = lax.Precision.HIGHEST
REACH = 14
NUGGET = 0.01
LENGTH = 0.8
LOG2E = math.log2(math.e)
LN2 = math.log(2.0)
ALPHA = math.sqrt(3.0) / LENGTH * LOG2E
X0 = ALPHA * ALPHA * NUGGET
VALUE_SCALE = LN2
SLOPE_SCALE = LN2 * LN2 / LENGTH
NODE_ROWS = 24
DEPTH = 4
CUTS = (4, 12, 24)
MIB = 2**20
AXES = ("group", "dev")


def dot(a, b):
    return jnp.dot(a, b, preferred_element_type=F32)


def dot32(a, b):
    return jnp.dot(a, b, preferred_element_type=F32, precision=HIGH)


def split2(x):
    hi = x.astype(BF)
    return hi, (x - hi.astype(F32)).astype(BF)


def split3(x):
    one = x.astype(BF).astype(F32)
    rest = x - one
    two = rest.astype(BF).astype(F32)
    return one, two, rest - two


def matern_terms(x):
    t = x * lax.rsqrt(x)
    e = jnp.exp2(-t)
    return (t + LOG2E) * e, x * e


def write_rows(rows, points, source):
    leaves = points[0].shape[0]
    spread = rows.shape[0] // 2

    def put(row, value):
        for h in range(2):
            rows[pl.ds(h * spread + row, leaves, stride=32), :] = value[:, 128 * h : 128 * h + 128]

    scaled = [p * (-2.0 * ALPHA if source else ALPHA) for p in points]
    square = scaled[0] * scaled[0] + scaled[1] * scaled[1] + scaled[2] * scaled[2]
    square = square * 0.25 if source else square + X0
    picks = (0, 1, 0, 1, 2, 0, 2, 1) if source else (0, 0, 1, 1, 0, 2, 1, 2)
    for c, value in enumerate(scaled):
        parts = split3(value)
        for r, pick in enumerate(picks):
            put(8 * c + r, parts[pick])
    one = jnp.ones_like(square)
    norms = split3(square)
    for r in range(3):
        put(24 + r, one if source else norms[r])
        put(27 + r, norms[r] if source else one)
        if r:
            put(29 + r, jnp.zeros_like(square))


def leaf_rows(rows, l):
    spread = rows.shape[0] // 2
    return [rows[pl.ds(h * spread + 32 * l, 32), :] for h in range(2)]


def write_source(wa, at, rows, l):
    for h, part in enumerate(leaf_rows(rows, l)):
        wa[at, 128 * h : 128 * h + 128, :] = jnp.transpose(part).astype(BF)


def node_block(charges, basis, leaf_transfer, dev_transfer, skeleton, out):
    total = jnp.zeros((32, 64), F32)
    for l in range(charges.shape[0]):
        leaf = lax.dot_general(
            charges[l], basis[l], (((1,), (1,)), ((), ())), precision=HIGH, preferred_element_type=F32
        )
        total += lax.dot_general(
            leaf, leaf_transfer[l], (((1,), (1,)), ((), ())), precision=HIGH, preferred_element_type=F32
        )
    image = lax.dot_general(
        total, dev_transfer[...], (((1,), (1,)), ((), ())), precision=HIGH, preferred_element_type=F32
    )
    out[0:16, :] = jnp.concatenate([total[:16], total[16:]], axis=1)
    out[16:24, :] = jnp.zeros((8, 128), F32)
    for c in range(3):
        out[16 + c : 17 + c, 0:64] = skeleton[c]
    out[24:40, :] = jnp.concatenate([image[:16], image[16:]], axis=1)


def prepare_kernel(reach, place, points_in, charges_in, neighbours_in, counts_in, basis_in, leaf_transfer_in, dev_transfer_in,
                   skeleton_in, up, down, packed, order, limits, block,
                   rows, points, charges, neighbours, counts, basis, leaf_transfer, dev_transfer, skeleton, sems):
    leaves, width = neighbours.shape
    sources = (points_in, charges_in, neighbours_in, counts_in, basis_in, leaf_transfer_in, dev_transfer_in, skeleton_in)
    targets = (points, charges, neighbours, counts, basis, leaf_transfer, dev_transfer, skeleton)
    loads = [pltpu.make_async_copy(a, b, sems.at[i]) for i, (a, b) in enumerate(zip(sources, targets))]
    for load in loads:
        load.start()
    loads[0].wait()
    coords = [points[c] for c in range(3)]
    for source in (True, False):
        write_rows(rows, coords, source)
        at = 0 if source else 32
        for l in range(leaves):
            packed[l, at : at + 32, :] = jnp.concatenate(leaf_rows(rows, l), axis=1).astype(BF)
    for ref, first in ((up, leaves - reach), (down, 0)):
        for c in range(3):
            at = 32 * reach + 16 * c
            ref[at : at + reach, :] = coords[c][first : first + reach]
            ref[at + reach : at + 16, :] = jnp.zeros((16 - reach, 256), F32)
    loads[1].wait()
    for l in range(leaves):
        packed[l, 64:96, :], packed[l, 96:128, :] = split2(charges[l])
        for ref, first in ((up, leaves - reach), (down, 0)):
            if 0 <= l - first < reach:
                ref[32 * (l - first) : 32 * (l - first) + 32, :] = charges[l]
    loads[2].wait()
    loads[3].wait()

    base = place[0] * leaves - reach

    def note(slot, at):
        for leaf in range(leaves):
            chosen = jnp.clip(neighbours[leaf, slot] - base, 0, leaves + 2 * reach - 1)
            order[at] = leaf * 64 + chosen
            at = at + (slot < counts[leaf]).astype(jnp.int32)
        return at

    ends = lax.fori_loop(0, width, note, 0)
    for k in range(DEPTH):
        order[ends + k] = leaves + 2 * reach
    limits[0] = (ends + DEPTH - 1) // DEPTH
    for load in loads[4:]:
        load.wait()
    node_block(charges, basis, leaf_transfer, dev_transfer, skeleton, block)


def merge_kernel(one, two, three, four, earlier, out):
    del earlier
    came = (one, two, three, four)
    count = one.shape[0] - 16
    for i, ref in enumerate(came):
        out[count * i : count * i + count, :] = ref[:count, :]
    out[4 * count :, :] = (one[count:, :] + two[count:, :]) + (three[count:, :] + four[count:, :])


def near_pairs(lo, hi, order, wa, c2, ua, acc, slots):
    xs, tiles = slots[:DEPTH], slots[DEPTH:]
    acc[...] = jnp.zeros_like(acc)
    tiles[DEPTH - 1][...] = jnp.zeros(tiles[0].shape, BF)

    def distances(i):
        pair = order[i]
        return dot(wa[pair % 64], ua[pair // 64])

    def gather_up(i, tile):
        pair = order[i]
        c, target = c2[pair % 64], pair // 64
        one, two = dot(c, tile[0]), dot(c[:32], tile[1])
        three, four = dot(c, tile[2]), dot(c[:32], tile[3])
        acc[target, 0:32, :] += one[:32] + two
        acc[target, 32:64, :] += one[32:]
        acc[target, 64:96, :] += three[:32] + four
        acc[target, 96:128, :] += three[32:]

    def step(i, b):
        xs[(b + 1) % DEPTH][...] = distances(jnp.minimum(i + 1, DEPTH * hi - 1))
        value, slope = matern_terms(xs[b][...])
        tiles[b][0], tiles[b][1] = split2(value)
        tiles[b][2], tiles[b][3] = split2(slope)
        gather_up(jnp.maximum(i - 1, DEPTH * lo), tiles[(b - 1) % DEPTH])

    def body(j, carry):
        for u in range(DEPTH):
            step(j * DEPTH + u, u)
        return carry

    @pl.when(jnp.asarray(hi > lo))
    def _():
        xs[0][...] = distances(DEPTH * lo)
        lax.fori_loop(lo, hi, body, 0)
        gather_up(DEPTH * hi - 1, tiles[DEPTH - 1])


def unpack(packed, offset, wa, c2):
    for l in range(packed.shape[0]):
        wa[offset + l] = jnp.transpose(packed[l, 0:32, :].astype(F32)).astype(BF)
        c2[offset + l] = packed[l, 64:128, :]


class Targets:
    def __init__(self, packed):
        self.packed = packed

    def __getitem__(self, i):
        return self.packed[i, 32:64, :]


class Selves:
    def __getitem__(self, i):
        return i * 65


def own_kernel(end, packed, earlier, acc, wa, c2, *slots):
    del earlier
    unpack(packed, 0, wa, c2)
    near_pairs(0, end, Selves(), wa, c2, Targets(packed), acc, slots)


def first_kernel(begin, end, order, limits, packed, before, after, earlier, acc, wa, c2, rows, *slots):
    del earlier
    leaves, half = packed.shape[0], before.shape[0] // 35
    total = leaves + 2 * half
    unpack(packed, half, wa, c2)
    for ref, offset in ((before, 0), (after, half + leaves)):
        write_rows(rows, [ref[32 * half + 16 * c : 32 * half + 16 * c + half, :] for c in range(3)], True)
        for l in range(half):
            write_source(wa, offset + l, rows, l)
            c2[offset + l, 0:32, :], c2[offset + l, 32:64, :] = split2(ref[32 * l : 32 * l + 32, :])
    wa[total] = wa[half]
    c2[total] = jnp.zeros(c2.shape[1:], BF)
    near_pairs(jnp.minimum(begin, limits[0]), jnp.minimum(end, limits[0]), order, wa, c2, Targets(packed), acc, slots)


def next_kernel(begin, end, order, limits, wa, c2, packed, earlier, acc, *slots):
    del earlier
    near_pairs(jnp.minimum(begin, limits[0]), jnp.minimum(end, limits[0]), order, wa, c2, Targets(packed), acc, slots)


def far_kernel(place, far_list, mine, theirs, own_skeleton, groups, dev_transfer, leaf_transfer, basis, near0, near1, near2, near3,
               value_out, slope_out, coefs, kernels):
    leaves = basis.shape[0]
    rank = place[0]
    group, node = rank // 64, rank % 64
    x0, z0, y0 = node % 4, (node // 4) % 4, node // 16

    def pair_kernel(column, row):
        x = jnp.full((64, 64), X0, F32)
        for c in range(3):
            d = (column[:, c : c + 1] - row[c : c + 1, :]) * ALPHA
            x = x + d * d
        value, slope = matern_terms(x)
        return jnp.concatenate([value * VALUE_SCALE, slope * SLOPE_SCALE], axis=1)

    own = jnp.concatenate([own_skeleton[c] for c in range(3)], axis=0)
    for j in range(far_list.shape[1]):
        s = far_list[0, j]
        d = s % 64
        jx, jz, jy = (x0 - d % 4 + 4) % 4, (z0 - (d // 4) % 4 + 4) % 4, (y0 - d // 16 + 4) % 4
        row = pl.multiple_of(((jx * 4 + jz) * 4 + jy) * NODE_ROWS, 8)
        block = jnp.where(s // 64 == group, mine[pl.ds(row, NODE_ROWS), :], theirs[pl.ds(row, NODE_ROWS), :])
        coefs[:, 64 * j : 64 * j + 64] = jnp.concatenate([block[:16, :64], block[:16, 64:]], axis=0)
        kernels[64 * j : 64 * j + 64, :] = pair_kernel(jnp.transpose(block[16:24, :])[:64], own)
    far = dot32(coefs[...], kernels[...])
    other = theirs[theirs.shape[0] - 16 :, :]
    other = jnp.concatenate([other[:, :64], other[:, 64:]], axis=0)
    near_group, far_group = groups[:, pl.ds(group, 1), :][:, 0], groups[:, pl.ds(1 - group, 1), :][:, 0]
    column = jnp.transpose(jnp.concatenate([far_group, jnp.zeros((5, 64), F32)], axis=0))
    top = dot32(other, pair_kernel(column, near_group))
    far = jnp.concatenate([far[:, :64], far[:, 64:]], axis=0)
    top = jnp.concatenate([top[:, :64], top[:, 64:]], axis=0)
    local_dev = far + dot32(top, dev_transfer[...])
    for l in range(leaves):
        part = dot32(dot32(local_dev, leaf_transfer[l]), basis[l])
        near = (near0[l] + near1[l]) + (near2[l] + near3[l])
        value_out[l] = (near[0:32] + near[32:64]) * VALUE_SCALE + part[:32]
        slope_out[l] = (near[64:96] + near[96:128]) * SLOPE_SCALE + part[32:]


VMEM = pl.BlockSpec(memory_space=pltpu.VMEM)
SMEM = pl.BlockSpec(memory_space=pltpu.SMEM)


def dev_shift(div, step):
    return [(i, i - (i // div) % 4 * div + ((i // div) % 4 + step) % 4 * div) for i in range(64)]


def local(points, charges, basis, leaf_transfer, dev_skeleton, dev_transfer, group_skeleton, neighbours, counts, far_list):
    leaves, width = neighbours.shape
    place = jnp.full((1,), lax.axis_index(AXES), jnp.int32)
    size = lax.axis_size(AXES)
    forward = [(i, i + 1) for i in range(size - 1)]
    anywhere = pl.BlockSpec(memory_space=pl.ANY)
    light = pl.CostEstimate(flops=1000, bytes_accessed=1000, transcendentals=0)

    def call(kernel, outs, ins, scratch, args, limit):
        return pl.pallas_call(
            kernel,
            out_shape=tuple(jax.ShapeDtypeStruct(shape, kind) for shape, kind in outs),
            in_specs=ins,
            out_specs=tuple(SMEM if kind == jnp.int32 else VMEM for _, kind in outs),
            scratch_shapes=scratch,
            compiler_params=pltpu.CompilerParams(vmem_limit_bytes=limit * MIB),
            cost_estimate=light,
        )(*args)

    def gathered(block, div, earlier):
        rows = 4 * block.shape[0] - 48
        came = [block] + [lax.ppermute(block, "dev", dev_shift(div, k)) for k in (1, 2, 3)]
        return call(merge_kernel, [((rows, 128), F32)], [VMEM] * 4 + [anywhere], [], (*came, earlier), 8)[0]

    points = jnp.transpose(points, (1, 0, 2))
    skeleton = jnp.transpose(dev_skeleton, (1, 0, 2))
    total = leaves + 2 * REACH
    strip = ((REACH * 32 + 48, 256), F32)
    rows = pltpu.VMEM((leaves * 64, 128), F32)
    held = (points, charges, neighbours, counts, basis, leaf_transfer, dev_transfer[0], skeleton)
    up, down, packed, order, limits, mine = call(
        lambda *refs: prepare_kernel(REACH, *refs),
        [strip, strip, ((leaves, 128, 256), BF),
         ((leaves * width + 2 * DEPTH,), jnp.int32), ((1,), jnp.int32), ((40, 128), F32)],
        [SMEM] + [pl.BlockSpec(memory_space=pltpu.HBM)] * 8,
        [rows] + [(pltpu.SMEM if h.dtype == jnp.int32 else pltpu.VMEM)(h.shape, h.dtype) for h in held]
        + [pltpu.SemaphoreType.DMA((8,))],
        (place, *held), 60,
    )
    before = lax.ppermute(up, AXES, forward)
    after = lax.ppermute(down, AXES, [(j, i) for i, j in forward])
    partial = ((leaves, 128, 256), F32)
    slots = [pltpu.VMEM((256, 256), F32)] * DEPTH + [pltpu.VMEM((4, 256, 256), BF)] * DEPTH
    (near0,) = call(
        lambda *refs: own_kernel(CUTS[0], *refs),
        [partial], [VMEM, anywhere], [pltpu.VMEM((leaves, 256, 32), BF), pltpu.VMEM((leaves, 64, 256), BF)] + slots,
        (packed, mine), 24,
    )
    mine = gathered(mine, 16, near0)
    near1, wa, c2 = call(
        lambda *refs: first_kernel(CUTS[0], CUTS[1], *refs),
        [partial, ((total + 1, 256, 32), BF), ((total + 1, 64, 256), BF)],
        [SMEM] * 2 + [VMEM] * 3 + [anywhere], [rows] + slots,
        (order, limits, packed, before, after, mine), 24,
    )
    mine = gathered(mine, 4, near1)
    (near2,) = call(
        lambda *refs: next_kernel(CUTS[1], CUTS[2], *refs),
        [partial], [SMEM] * 2 + [VMEM] * 3 + [anywhere], slots, (order, limits, wa, c2, packed, mine), 24,
    )
    mine = gathered(mine, 1, near2)
    theirs = lax.ppermute(mine, "group", [(0, 1), (1, 0)])
    (near3,) = call(
        lambda *refs: next_kernel(CUTS[2], leaves * width, *refs),
        [partial], [SMEM] * 2 + [VMEM] * 3 + [anywhere], slots, (order, limits, wa, c2, packed, mine), 24,
    )
    out = ((leaves, 32, 256), F32)
    return call(
        far_kernel, [out, out], [SMEM] * 2 + [VMEM] * 11,
        [pltpu.VMEM((32, 1024), F32), pltpu.VMEM((1024, 128), F32)],
        (place, far_list, mine, theirs, skeleton, jnp.transpose(group_skeleton, (1, 0, 2)), dev_transfer[0],
         leaf_transfer, basis, near0, near1, near2, near3), 24,
    )


def solution(mesh):
    leaf = P(AXES, None, None)
    placed = (leaf, leaf, leaf, leaf, leaf, leaf, P(), P(AXES, None), P(AXES), P(AXES, None))
    return jax.shard_map(local, mesh=mesh, in_specs=placed, out_specs=(leaf, leaf), check_vma=False)
```

```python
import math

import jax
import jax.numpy as jnp
from jax import lax
from jax.experimental import pallas as pl
from jax.experimental.pallas import tpu as pltpu
from jax.sharding import PartitionSpec as P

BF = jnp.bfloat16
F32 = jnp.float32
HIGH = lax.Precision.HIGHEST
REACH = 14
NUGGET = 0.01
LENGTH = 0.8
LOG2E = math.log2(math.e)
LN2 = math.log(2.0)
ALPHA = math.sqrt(3.0) / LENGTH * LOG2E
X0 = ALPHA * ALPHA * NUGGET
VALUE_SCALE = LN2
SLOPE_SCALE = LN2 * LN2 / LENGTH
NODE_ROWS = 24
LIFT = 6
CHARGE_LIFT = 14
F8 = jnp.float8_e5m2
DEPTH = 8
CUTS = (2, 6, 12)
MIB = 2**20
AXES = ("group", "dev")


def dot(a, b):
    return jnp.dot(a, b, preferred_element_type=F32)


def dot32(a, b):
    return jnp.dot(a, b, preferred_element_type=F32, precision=HIGH)


def split2(x):
    hi = x.astype(BF)
    return hi, (x - hi.astype(F32)).astype(BF)


def split3(x):
    one = x.astype(BF).astype(F32)
    rest = x - one
    two = rest.astype(BF).astype(F32)
    return one, two, rest - two


def matern_terms(x, lift=0):
    t = x * lax.rsqrt(x)
    e = jnp.exp2(lift - t)
    return (t + LOG2E) * e, x * e


def write_rows(rows, points, source):
    leaves = points[0].shape[0]
    spread = rows.shape[0] // 2

    def put(row, value):
        for h in range(2):
            rows[pl.ds(h * spread + row, leaves, stride=32), :] = value[:, 128 * h : 128 * h + 128]

    scaled = [p * (-2.0 * ALPHA if source else ALPHA) for p in points]
    square = scaled[0] * scaled[0] + scaled[1] * scaled[1] + scaled[2] * scaled[2]
    square = square * 0.25 if source else square + X0
    picks = (0, 1, 0, 1, 2, 0, 2, 1) if source else (0, 0, 1, 1, 0, 2, 1, 2)
    for c, value in enumerate(scaled):
        parts = split3(value)
        for r, pick in enumerate(picks):
            put(8 * c + r, parts[pick])
    one = jnp.ones_like(square)
    norms = split3(square)
    for r in range(3):
        put(24 + r, one if source else norms[r])
        put(27 + r, norms[r] if source else one)
        if r:
            put(29 + r, jnp.zeros_like(square))


def leaf_rows(rows, l):
    spread = rows.shape[0] // 2
    return [rows[pl.ds(h * spread + 32 * l, 32), :] for h in range(2)]


def write_source(wa, at, rows, l):
    for h, part in enumerate(leaf_rows(rows, l)):
        wa[at, 128 * h : 128 * h + 128, :] = jnp.transpose(part).astype(BF)


def dot_t(a, b):
    return lax.dot_general(a, b, (((1,), (1,)), ((), ())), preferred_element_type=F32)


def node_block(packed, basis, leaf_transfer, dev_transfer, skeleton, product, out):
    high, low = jnp.zeros((64, 64), F32), jnp.zeros((32, 64), F32)
    for l in range(basis.shape[0]):
        left, left_low = split2(leaf_transfer[l])
        right, right_low = split2(basis[l])
        both = dot(jnp.concatenate([left, left_low], axis=0), right)
        one, two = split2(both[:64] + both[64:] + dot(left, right_low))
        product[l, 0:64, :], product[l, 64:128, :] = one, two
        high += dot_t(packed[l, 64:128, :], one)
        low += dot_t(packed[l, 64:96, :], two)
    total = high[:32] + high[32:] + low
    image = lax.dot_general(
        total, dev_transfer[...], (((1,), (1,)), ((), ())), precision=HIGH, preferred_element_type=F32
    )
    out[0:16, :] = jnp.concatenate([total[:16], total[16:]], axis=1)
    out[16:24, :] = jnp.zeros((8, 128), F32)
    for c in range(3):
        out[16 + c : 17 + c, 0:64] = skeleton[c]
    out[24:40, :] = jnp.concatenate([image[:16], image[16:]], axis=1)


def prepare_kernel(reach, place, points_in, charges_in, neighbours_in, counts_in, basis_in, leaf_transfer_in, dev_transfer_in,
                   skeleton_in, up, down, packed, order, limits, block, product,
                   rows, points, charges, neighbours, counts, basis, leaf_transfer, dev_transfer, skeleton, sems):
    leaves, width = neighbours.shape
    sources = (points_in, charges_in, neighbours_in, counts_in, basis_in, leaf_transfer_in, dev_transfer_in, skeleton_in)
    targets = (points, charges, neighbours, counts, basis, leaf_transfer, dev_transfer, skeleton)
    loads = [pltpu.make_async_copy(a, b, sems.at[i]) for i, (a, b) in enumerate(zip(sources, targets))]
    for load in loads:
        load.start()
    loads[0].wait()
    coords = [points[c] for c in range(3)]
    for source in (True, False):
        write_rows(rows, coords, source)
        at = 0 if source else 32
        for l in range(leaves):
            packed[l, at : at + 32, :] = jnp.concatenate(leaf_rows(rows, l), axis=1).astype(BF)
    for ref, first in ((up, leaves - reach), (down, 0)):
        for c in range(3):
            at = 32 * reach + 16 * c
            ref[at : at + reach, :] = coords[c][first : first + reach]
            ref[at + reach : at + 16, :] = jnp.zeros((16 - reach, 256), F32)
    loads[1].wait()
    for l in range(leaves):
        packed[l, 64:96, :], packed[l, 96:128, :] = split2(charges[l])
        for ref, first in ((up, leaves - reach), (down, 0)):
            if 0 <= l - first < reach:
                ref[32 * (l - first) : 32 * (l - first) + 32, :] = charges[l]
    loads[2].wait()
    loads[3].wait()

    base = place[0] * leaves - reach

    def note(slot, at):
        for leaf in range(leaves):
            chosen = jnp.clip(neighbours[leaf, slot] - base, 0, leaves + 2 * reach - 1)
            order[at] = leaf * 64 + chosen
            at = at + (slot < counts[leaf]).astype(jnp.int32)
        return at

    ends = lax.fori_loop(0, width, note, 0)
    for k in range(DEPTH):
        order[ends + k] = leaves + 2 * reach
    limits[0] = (ends + DEPTH - 1) // DEPTH
    for load in loads[4:]:
        load.wait()
    node_block(packed, basis, leaf_transfer, dev_transfer, skeleton, product, block)


def merge_kernel(one, two, three, four, earlier, out):
    del earlier
    count = one.shape[0] - 16
    for i, ref in enumerate((one, two, three, four)):
        out[count * i : count * i + count, :] = ref[:count, :]
    out[4 * count :, :] = (one[count:, :] + two[count:, :]) + (three[count:, :] + four[count:, :])


def near_pairs(lo, hi, order, wa, c2, c8, ua, acc, slots):
    xs, highs, lows = slots[:DEPTH], slots[DEPTH : 2 * DEPTH], slots[2 * DEPTH :]
    acc[...] = jnp.zeros_like(acc)
    highs[DEPTH - 1][...] = jnp.zeros(highs[0].shape, BF)
    lows[DEPTH - 1][...] = jnp.zeros(lows[0].shape, F8)

    def distances(i):
        pair = order[i]
        return dot(wa[pair % 64], ua[pair // 64])

    def gather_up(i, b):
        pair = order[i]
        c, small, target = c2[pair % 64], c8[pair % 64], pair // 64
        one, two = dot(c, highs[b][0]), dot(small, lows[b][0]) * 2.0**-CHARGE_LIFT
        three, four = dot(c, highs[b][1]), dot(small, lows[b][1]) * 2.0**-CHARGE_LIFT
        acc[target, 0:32, :] += one[:32] + two
        acc[target, 32:64, :] += one[32:]
        acc[target, 64:96, :] += three[:32] + four
        acc[target, 96:128, :] += three[32:]

    def step(i, b):
        xs[(b + 1) % DEPTH][...] = distances(jnp.minimum(i + 1, DEPTH * hi - 1))
        for k, term in enumerate(matern_terms(xs[b][...], LIFT)):
            high = term.astype(BF)
            highs[b][k] = high
            lows[b][k] = (term - high.astype(F32)).astype(F8)
        gather_up(jnp.maximum(i - 1, DEPTH * lo), (b - 1) % DEPTH)

    def body(j, carry):
        for u in range(DEPTH):
            step(j * DEPTH + u, u)
        return carry

    @pl.when(jnp.asarray(hi > lo))
    def _():
        xs[0][...] = distances(DEPTH * lo)
        lax.fori_loop(lo, hi, body, 0)
        gather_up(DEPTH * hi - 1, DEPTH - 1)


def small_charges(high):
    return (high.astype(F32) * 2.0**CHARGE_LIFT).astype(F8)


def unpack(packed, wa, c2, c8, offset):
    for l in range(packed.shape[0]):
        wa[offset + l] = jnp.transpose(packed[l, 0:32, :].astype(F32)).astype(BF)
        c2[offset + l] = packed[l, 64:128, :]
        c8[offset + l] = small_charges(packed[l, 64:96, :])


class Targets:
    def __init__(self, packed):
        self.packed = packed

    def __getitem__(self, i):
        return self.packed[i, 32:64, :]


class Selves:
    def __getitem__(self, i):
        return i * 65


def own_kernel(end, packed, earlier, acc, wa, c2, c8, *slots):
    del earlier
    unpack(packed, wa, c2, c8, 0)
    near_pairs(0, end, Selves(), wa, c2, c8, Targets(packed), acc, slots)


def first_kernel(begin, end, order, limits, packed, before, after, earlier, acc, wa, c2, c8, rows, *slots):
    del earlier
    leaves, half = packed.shape[0], before.shape[0] // 35
    total = leaves + 2 * half
    unpack(packed, wa, c2, c8, half)
    for ref, offset in ((before, 0), (after, half + leaves)):
        write_rows(rows, [ref[32 * half + 16 * c : 32 * half + 16 * c + half, :] for c in range(3)], True)
        for l in range(half):
            write_source(wa, offset + l, rows, l)
            high, low = split2(ref[32 * l : 32 * l + 32, :])
            c2[offset + l, 0:32, :], c2[offset + l, 32:64, :] = high, low
            c8[offset + l] = small_charges(high)
    wa[total] = wa[half]
    c2[total] = jnp.zeros(c2.shape[1:], BF)
    c8[total] = jnp.zeros(c8.shape[1:], F8)
    near_pairs(jnp.minimum(begin, limits[0]), jnp.minimum(end, limits[0]), order, wa, c2, c8, Targets(packed), acc, slots)


def next_kernel(begin, end, order, limits, wa, c2, c8, packed, earlier, acc, *slots):
    del earlier
    near_pairs(jnp.minimum(begin, limits[0]), jnp.minimum(end, limits[0]), order, wa, c2, c8, Targets(packed), acc, slots)


def far_kernel(place, far_list, mine, theirs, own_skeleton, groups, dev_transfer, product, *refs):
    nears, (value_out, slope_out, coefs, kernels) = refs[:-4], refs[-4:]
    leaves = product.shape[0]
    rank = place[0]
    group, node = rank // 64, rank % 64

    def pair_kernel(column, row):
        x = jnp.full((64, 64), X0, F32)
        for c in range(3):
            d = (column[:, c : c + 1] - row[c : c + 1, :]) * ALPHA
            x = x + d * d
        value, slope = matern_terms(x)
        return jnp.concatenate([value * VALUE_SCALE, slope * SLOPE_SCALE], axis=1)

    own = jnp.concatenate([own_skeleton[c] for c in range(3)], axis=0)
    for j in range(far_list.shape[1]):
        s = far_list[0, j]
        x, z, y = node - s, node // 4 - s % 64 // 4, node // 16 - s % 64 // 16
        row = pl.multiple_of(((x & 3) * 16 + (z & 3) * 4 + (y & 3)) * NODE_ROWS, 8)
        block = jnp.where(s // 64 == group, mine[pl.ds(row, NODE_ROWS), :], theirs[pl.ds(row, NODE_ROWS), :])
        coefs[:, 64 * j : 64 * j + 64] = jnp.concatenate([block[:16, :64], block[:16, 64:]], axis=0)
        kernels[64 * j : 64 * j + 64, :] = pair_kernel(jnp.transpose(block[16:24, :])[:64], own)
    coef, coef_low = split2(coefs[...])
    kernel, kernel_low = split2(kernels[...])
    both = dot(jnp.concatenate([coef, coef_low], axis=0), kernel)
    far = both[:32] + both[32:] + dot(coef, kernel_low)
    other = theirs[theirs.shape[0] - 16 :, :]
    other = jnp.concatenate([other[:, :64], other[:, 64:]], axis=0)
    near_group, far_group = groups[:, pl.ds(group, 1), :][:, 0], groups[:, pl.ds(1 - group, 1), :][:, 0]
    column = jnp.transpose(jnp.concatenate([far_group, jnp.zeros((5, 64), F32)], axis=0))
    top = dot32(other, pair_kernel(column, near_group))
    far = jnp.concatenate([far[:, :64], far[:, 64:]], axis=0)
    top = jnp.concatenate([top[:, :64], top[:, 64:]], axis=0)
    local_dev, local_low = split2(far + dot32(top, dev_transfer[...]))
    local_both = jnp.concatenate([local_dev, local_low], axis=0)
    for l in range(leaves):
        both = dot(local_both, product[l, 0:64, :])
        part = both[:64] + both[64:] + dot(local_dev, product[l, 64:128, :])
        near = (nears[0][l] + nears[1][l]) + (nears[2][l] + nears[3][l])
        value_out[l] = (near[0:32] + near[32:64]) * (VALUE_SCALE * 2.0**-LIFT) + part[:32]
        slope_out[l] = (near[64:96] + near[96:128]) * (SLOPE_SCALE * 2.0**-LIFT) + part[32:]


VMEM = pl.BlockSpec(memory_space=pltpu.VMEM)
SMEM = pl.BlockSpec(memory_space=pltpu.SMEM)


def dev_shift(div, step):
    return [(i, i - (i // div) % 4 * div + ((i // div) % 4 + step) % 4 * div) for i in range(64)]


def local(points, charges, basis, leaf_transfer, dev_skeleton, dev_transfer, group_skeleton, neighbours, counts, far_list):
    leaves, width = neighbours.shape
    place = jnp.full((1,), lax.axis_index(AXES), jnp.int32)
    size = lax.axis_size(AXES)
    forward = [(i, i + 1) for i in range(size - 1)]
    anywhere = pl.BlockSpec(memory_space=pl.ANY)
    light = pl.CostEstimate(flops=1000, bytes_accessed=1000, transcendentals=0)

    def call(kernel, outs, ins, scratch, args, limit):
        return pl.pallas_call(
            kernel,
            out_shape=tuple(jax.ShapeDtypeStruct(shape, kind) for shape, kind in outs),
            in_specs=ins,
            out_specs=tuple(SMEM if kind == jnp.int32 else VMEM for _, kind in outs),
            scratch_shapes=scratch,
            compiler_params=pltpu.CompilerParams(vmem_limit_bytes=limit * MIB),
            cost_estimate=light,
        )(*args)

    def gathered(block, div, earlier):
        rows = 4 * block.shape[0] - 48
        came = [block] + [lax.ppermute(block, "dev", dev_shift(div, k)) for k in (1, 3, 2)]
        came = [came[0], came[1], came[3], came[2]]
        return call(merge_kernel, [((rows, 128), F32)], [VMEM] * 4 + [anywhere], [], (*came, earlier), 8)[0]

    points = jnp.transpose(points, (1, 0, 2))
    skeleton = jnp.transpose(dev_skeleton, (1, 0, 2))
    total = leaves + 2 * REACH
    strip = ((REACH * 32 + 48, 256), F32)
    rows = pltpu.VMEM((leaves * 64, 128), F32)
    held = (points, charges, neighbours, counts, basis, leaf_transfer, dev_transfer[0], skeleton)
    up, down, packed, order, limits, mine, product = call(
        lambda *refs: prepare_kernel(REACH, *refs),
        [strip, strip, ((leaves, 128, 256), BF),
         ((leaves * width + 2 * DEPTH,), jnp.int32), ((1,), jnp.int32), ((40, 128), F32), ((leaves, 128, 256), BF)],
        [SMEM] + [pl.BlockSpec(memory_space=pltpu.HBM)] * 8,
        [rows] + [(pltpu.SMEM if h.dtype == jnp.int32 else pltpu.VMEM)(h.shape, h.dtype) for h in held]
        + [pltpu.SemaphoreType.DMA((8,))],
        (place, *held), 60,
    )
    before = lax.ppermute(up, AXES, forward)
    after = lax.ppermute(down, AXES, [(j, i) for i, j in forward])
    partial = ((leaves, 128, 256), F32)
    slots = [pltpu.VMEM((256, 256), F32)] * DEPTH + [pltpu.VMEM((2, 256, 256), BF)] * DEPTH
    slots += [pltpu.VMEM((2, 256, 256), F8)] * DEPTH
    sources = [((leaves, 256, 32), BF), ((leaves, 64, 256), BF), ((leaves, 32, 256), F8)]
    (near0,) = call(
        lambda *refs: own_kernel(CUTS[0], *refs),
        [partial], [VMEM, anywhere], [pltpu.VMEM(*source) for source in sources] + slots, (packed, mine), 24,
    )
    mine = gathered(mine, 16, near0)
    near1, *held = call(
        lambda *refs: first_kernel(CUTS[0], CUTS[1], *refs),
        [partial] + [((total + 1, *shape[1:]), kind) for shape, kind in sources],
        [SMEM] * 2 + [VMEM] * 3 + [anywhere], [rows] + slots,
        (order, limits, packed, before, after, mine), 24,
    )
    mine = gathered(mine, 4, near1)
    (near2,) = call(
        lambda *refs: next_kernel(CUTS[1], CUTS[2], *refs),
        [partial], [SMEM] * 2 + [VMEM] * 4 + [anywhere], slots, (order, limits, *held, packed, mine), 24,
    )
    mine = gathered(mine, 1, near2)
    theirs = lax.ppermute(mine, "group", [(0, 1), (1, 0)])
    (near3,) = call(
        lambda *refs: next_kernel(CUTS[2], leaves * width // DEPTH, *refs),
        [partial], [SMEM] * 2 + [VMEM] * 4 + [anywhere], slots, (order, limits, *held, packed, mine), 24,
    )
    nears = (near0, near1, near2, near3)
    out = ((leaves, 32, 256), F32)
    return call(
        far_kernel, [out, out], [SMEM] * 2 + [VMEM] * (6 + len(nears)),
        [pltpu.VMEM((32, 1024), F32), pltpu.VMEM((1024, 128), F32)],
        (place, far_list, mine, theirs, skeleton, jnp.transpose(group_skeleton, (1, 0, 2)), dev_transfer[0],
         product, *nears), 24,
    )


def solution(mesh):
    leaf = P(AXES, None, None)
    placed = (leaf, leaf, leaf, leaf, leaf, leaf, P(), P(AXES, None), P(AXES), P(AXES, None))
    return jax.shard_map(local, mesh=mesh, in_specs=placed, out_specs=(leaf, leaf), check_vma=False)
```

```python
import math

import jax
import jax.numpy as jnp
from jax import lax
from jax.experimental import pallas as pl
from jax.experimental.pallas import tpu as pltpu
from jax.sharding import PartitionSpec as P

BF = jnp.bfloat16
F32 = jnp.float32
HIGH = lax.Precision.HIGHEST
REACH = 14
NUGGET = 0.01
LENGTH = 0.8
LOG2E = math.log2(math.e)
LN2 = math.log(2.0)
ALPHA = math.sqrt(3.0) / LENGTH * LOG2E
X0 = ALPHA * ALPHA * NUGGET
VALUE_SCALE = LN2
SLOPE_SCALE = LN2 * LN2 / LENGTH
NODE_ROWS = 24
LIFT = 6
CHARGE_LIFT = 14
F8 = jnp.float8_e5m2
DEPTH = 8
CUTS = (2, 6, 12)
MIB = 2**20
AXES = ("group", "dev")


def my_rank():
    return lax.axis_index("group") * 64 + lax.axis_index("dev")


def dot(a, b):
    return jnp.dot(a, b, preferred_element_type=F32)


def dot32(a, b):
    return jnp.dot(a, b, preferred_element_type=F32, precision=HIGH)


def split2(x):
    hi = x.astype(BF)
    return hi, (x - hi.astype(F32)).astype(BF)


def split3(x):
    one = x.astype(BF).astype(F32)
    rest = x - one
    two = rest.astype(BF).astype(F32)
    return one, two, rest - two


def matern_terms(x, lift=0):
    t = x * lax.rsqrt(x)
    e = jnp.exp2(lift - t)
    return (t + LOG2E) * e, x * e


def write_rows(rows, points, source):
    leaves = points[0].shape[0]
    spread = rows.shape[0] // 2

    def put(row, value):
        for h in range(2):
            rows[pl.ds(h * spread + row, leaves, stride=32), :] = value[:, 128 * h : 128 * h + 128]

    scaled = [p * (-2.0 * ALPHA if source else ALPHA) for p in points]
    square = scaled[0] * scaled[0] + scaled[1] * scaled[1] + scaled[2] * scaled[2]
    square = square * 0.25 if source else square + X0
    picks = (0, 1, 0, 1, 2, 0, 2, 1) if source else (0, 0, 1, 1, 0, 2, 1, 2)
    for c, value in enumerate(scaled):
        parts = split3(value)
        for r, pick in enumerate(picks):
            put(8 * c + r, parts[pick])
    one = jnp.ones_like(square)
    norms = split3(square)
    for r in range(3):
        put(24 + r, one if source else norms[r])
        put(27 + r, norms[r] if source else one)
        if r:
            put(29 + r, jnp.zeros_like(square))


def leaf_rows(rows, l):
    spread = rows.shape[0] // 2
    return [rows[pl.ds(h * spread + 32 * l, 32), :] for h in range(2)]


def write_source(wa, at, rows, l):
    for h, part in enumerate(leaf_rows(rows, l)):
        wa[at, 128 * h : 128 * h + 128, :] = jnp.transpose(part).astype(BF)


def dot_t(a, b):
    return lax.dot_general(a, b, (((1,), (1,)), ((), ())), preferred_element_type=F32)


def node_block(packed, basis, leaf_transfer, dev_transfer, skeleton, product, out, meanwhile):
    high, low = jnp.zeros((64, 64), F32), jnp.zeros((32, 64), F32)
    for l in range(basis.shape[0]):
        left, left_low = split2(leaf_transfer[l])
        right, right_low = split2(basis[l])
        both = dot(jnp.concatenate([left, left_low], axis=0), right)
        one, two = split2(both[:64] + both[64:] + dot(left, right_low))
        product[l, 0:64, :], product[l, 64:128, :] = one, two
        high += dot_t(packed[l, 64:128, :], one)
        low += dot_t(packed[l, 64:96, :], two)
    meanwhile()
    total = high[:32] + high[32:] + low
    image = lax.dot_general(
        total, dev_transfer[...], (((1,), (1,)), ((), ())), precision=HIGH, preferred_element_type=F32
    )
    out[0:16, :] = jnp.concatenate([total[:16], total[16:]], axis=1)
    out[16:24, :] = jnp.zeros((8, 128), F32)
    for c in range(3):
        out[16 + c : 17 + c, 0:64] = skeleton[c]
    out[24:40, :] = jnp.concatenate([image[:16], image[16:]], axis=1)


def prepare_kernel(reach, points_in, charges_in, neighbours_in, counts_in, basis_in, leaf_transfer_in, dev_transfer_in,
                   skeleton_in, up, down, packed_out, product_out, order_out, block,
                   rows, edges, packed, product, points, charges, neighbours, counts, basis, leaf_transfer, dev_transfer,
                   skeleton, order, load_sems, store_sems):
    leaves, width = neighbours.shape
    sources = (points_in, charges_in, neighbours_in, counts_in, basis_in, leaf_transfer_in, dev_transfer_in, skeleton_in)
    targets = (points, charges, neighbours, counts, basis, leaf_transfer, dev_transfer, skeleton)
    loads = [pltpu.make_async_copy(a, b, load_sems.at[i]) for i, (a, b) in enumerate(zip(sources, targets))]
    for load in loads:
        load.start()
    stores = []

    def store(source, target):
        stores.append(pltpu.make_async_copy(source, target, store_sems.at[len(stores)]))
        stores[-1].start()

    moved = 32 * reach
    loads[0].wait()
    coords = [points[c] for c in range(3)]
    for i, first in enumerate((leaves - reach, 0)):
        for c in range(3):
            edges[i, 16 * c : 16 * c + reach, :] = coords[c][first : first + reach]
            edges[i, 16 * c + reach : 16 * c + 16, :] = jnp.zeros((16 - reach, 256), F32)
        store(edges.at[i], (up, down)[i].at[pl.ds(moved, 48)])
    for source in (True, False):
        write_rows(rows, coords, source)
        at = 0 if source else 32
        for l in range(leaves):
            packed[l, at : at + 32, :] = jnp.concatenate(leaf_rows(rows, l), axis=1).astype(BF)
    loads[1].wait()
    store(charges.at[pl.ds(32 * (leaves - reach), moved)], up.at[pl.ds(0, moved)])
    store(charges.at[pl.ds(0, moved)], down.at[pl.ds(0, moved)])
    for l in range(leaves):
        packed[l, 64:96, :], packed[l, 96:128, :] = split2(charges[32 * l : 32 * l + 32, :])
    store(packed, packed_out)
    for load in loads[4:]:
        load.wait()

    def listing():
        store(product, product_out)
        loads[2].wait()
        loads[3].wait()
        base = my_rank() * leaves - reach

        def note(slot, at):
            for leaf in range(leaves):
                chosen = jnp.clip(neighbours[leaf, slot] - base, 0, leaves + 2 * reach - 1)
                order[at] = leaf * 64 + chosen
                at = at + (slot < counts[leaf]).astype(jnp.int32)
            return at

        ends = lax.fori_loop(0, width, note, 0)
        for k in range(DEPTH):
            order[ends + k] = leaves + 2 * reach
        order[order.shape[0] - 1] = (ends + DEPTH - 1) // DEPTH
        store(order, order_out)

    node_block(packed, basis, leaf_transfer, dev_transfer, skeleton, product, block, listing)
    for one in stores:
        one.wait()


def merge_kernel(shifts, own, one, two, three, earlier, out):
    del earlier
    count = one.shape[0] - 16
    for i, ref in zip((0, *shifts), (own, one, two, three)):
        out[count * i : count * i + count, :] = ref[:count, :]
    out[4 * count :, :] = (own[count:, :] + one[count:, :]) + (two[count:, :] + three[count:, :])


def near_pairs(lo, hi, order, wa, c2, c8, ua, start, acc, slots, load=None):
    xs, highs, lows = slots[:DEPTH], slots[DEPTH : 2 * DEPTH], slots[2 * DEPTH :]

    def begin(l, carry):
        acc[l] = jnp.zeros(acc.shape[1:], F32) if start is None else start[l]
        return carry

    lax.fori_loop(0, acc.shape[0], begin, 0)
    highs[DEPTH - 1][...] = jnp.zeros(highs[0].shape, BF)
    lows[DEPTH - 1][...] = jnp.zeros(lows[0].shape, F8)
    if load is not None:
        load.wait()
        last = order[order.shape[0] - 1]
        lo, hi = jnp.minimum(lo, last), jnp.minimum(hi, last)

    def distances(i):
        pair = order[i]
        return dot(wa[pair % 64], ua[pair // 64])

    def gather_up(i, b):
        pair = order[i]
        c, small, target = c2[pair % 64], c8[pair % 64], pair // 64
        one, two = dot(c, highs[b][0]), dot(small, lows[b][0]) * 2.0**-CHARGE_LIFT
        three, four = dot(c, highs[b][1]), dot(small, lows[b][1]) * 2.0**-CHARGE_LIFT
        acc[target, 0:32, :] += one[:32] + two
        acc[target, 32:64, :] += one[32:]
        acc[target, 64:96, :] += three[:32] + four
        acc[target, 96:128, :] += three[32:]

    def step(i, b):
        xs[(b + 1) % DEPTH][...] = distances(jnp.minimum(i + 1, DEPTH * hi - 1))
        for k, term in enumerate(matern_terms(xs[b][...], LIFT)):
            high = term.astype(BF)
            highs[b][k] = high
            lows[b][k] = (term - high.astype(F32)).astype(F8)
        gather_up(jnp.maximum(i - 1, DEPTH * lo), (b - 1) % DEPTH)

    def body(j, carry):
        for u in range(DEPTH):
            step(j * DEPTH + u, u)
        return carry

    @pl.when(jnp.asarray(hi > lo))
    def _():
        xs[0][...] = distances(DEPTH * lo)
        lax.fori_loop(lo, hi, body, 0)
        gather_up(DEPTH * hi - 1, DEPTH - 1)


def small_charges(high):
    return (high.astype(F32) * 2.0**CHARGE_LIFT).astype(F8)


def unpack(packed, wa, c2, c8, offset):
    for l in range(packed.shape[0]):
        wa[offset + l] = jnp.transpose(packed[l, 0:32, :].astype(F32)).astype(BF)
        c2[offset + l] = packed[l, 64:128, :]
        c8[offset + l] = small_charges(packed[l, 64:96, :])


class Targets:
    def __init__(self, packed):
        self.packed = packed

    def __getitem__(self, i):
        return self.packed[i, 32:64, :]


class Selves:
    def __getitem__(self, i):
        return i * 65


def own_kernel(end, packed, earlier, acc, wa, c2, c8, *slots):
    del earlier
    unpack(packed, wa, c2, c8, 0)
    near_pairs(0, end, Selves(), wa, c2, c8, Targets(packed), None, acc, slots)


def first_kernel(begin, end, order_in, packed, before, after, start, earlier, acc, wa, c2, c8, rows, order, sem, *slots):
    del earlier
    load = pltpu.make_async_copy(order_in, order, sem)
    load.start()
    leaves, half = packed.shape[0], before.shape[0] // 35
    total = leaves + 2 * half
    unpack(packed, wa, c2, c8, half)
    for ref, offset in ((before, 0), (after, half + leaves)):
        write_rows(rows, [ref[32 * half + 16 * c : 32 * half + 16 * c + half, :] for c in range(3)], True)
        for l in range(half):
            write_source(wa, offset + l, rows, l)
            high, low = split2(ref[32 * l : 32 * l + 32, :])
            c2[offset + l, 0:32, :], c2[offset + l, 32:64, :] = high, low
            c8[offset + l] = small_charges(high)
    wa[total] = wa[half]
    c2[total] = jnp.zeros(c2.shape[1:], BF)
    c8[total] = jnp.zeros(c8.shape[1:], F8)
    near_pairs(begin, end, order, wa, c2, c8, Targets(packed), start, acc, slots, load)


def next_kernel(begin, end, order_in, wa, c2, c8, packed, start, earlier, acc, order, sem, *slots):
    del earlier
    load = pltpu.make_async_copy(order_in, order, sem)
    load.start()
    near_pairs(begin, end, order, wa, c2, c8, Targets(packed), start, acc, slots, load)


def far_kernel(far_list_in, mine, theirs, own_skeleton, groups, dev_transfer, product, near, value_out, slope_out,
               coefs, kernels, values, slopes, far_list, load_sem, sems):
    load = pltpu.make_async_copy(far_list_in, far_list, load_sem)
    load.start()
    leaves = product.shape[0]
    group, node = lax.axis_index("group"), lax.axis_index("dev")

    def pair_kernel(column, row):
        x = jnp.full((64, 64), X0, F32)
        for c in range(3):
            d = (column[:, c : c + 1] - row[c : c + 1, :]) * ALPHA
            x = x + d * d
        value, slope = matern_terms(x)
        return jnp.concatenate([value * VALUE_SCALE, slope * SLOPE_SCALE], axis=1)

    other = theirs[theirs.shape[0] - 16 :, :]
    other = jnp.concatenate([other[:, :64], other[:, 64:]], axis=0)
    near_group, far_group = groups[:, pl.ds(group, 1), :][:, 0], groups[:, pl.ds(1 - group, 1), :][:, 0]
    column = jnp.transpose(jnp.concatenate([far_group, jnp.zeros((5, 64), F32)], axis=0))
    top = dot32(other, pair_kernel(column, near_group))
    top = jnp.concatenate([top[:, :64], top[:, 64:]], axis=0)
    top = dot32(top, dev_transfer[...])
    load.wait()
    own = jnp.concatenate([own_skeleton[c] for c in range(3)], axis=0)
    for j in range(far_list.shape[1]):
        s = far_list[0, j]
        x, z, y = node - s, node // 4 - s % 64 // 4, node // 16 - s % 64 // 16
        row = pl.multiple_of(((x & 3) * 16 + (z & 3) * 4 + (y & 3)) * NODE_ROWS, 8)
        block = jnp.where(s // 64 == group, mine[pl.ds(row, NODE_ROWS), :], theirs[pl.ds(row, NODE_ROWS), :])
        coefs[:, 64 * j : 64 * j + 64] = jnp.concatenate([block[:16, :64], block[:16, 64:]], axis=0)
        kernels[64 * j : 64 * j + 64, :] = pair_kernel(jnp.transpose(block[16:24, :])[:64], own)
    coef, coef_low = split2(coefs[...])
    kernel, kernel_low = split2(kernels[...])
    both = dot(jnp.concatenate([coef, coef_low], axis=0), kernel)
    far = both[:32] + both[32:] + dot(coef, kernel_low)
    far = jnp.concatenate([far[:, :64], far[:, 64:]], axis=0)
    local_dev, local_low = split2(far + top)
    local_both = jnp.concatenate([local_dev, local_low], axis=0)
    stores = []
    for l in range(leaves):
        both = dot(local_both, product[l, 0:64, :])
        part = both[:64] + both[64:] + dot(local_dev, product[l, 64:128, :])
        both = near[l]
        values[l] = (both[0:32] + both[32:64]) * (VALUE_SCALE * 2.0**-LIFT) + part[:32]
        slopes[l] = (both[64:96] + both[96:128]) * (SLOPE_SCALE * 2.0**-LIFT) + part[32:]
        if l % 4 == 3:
            some = slice(l - 3, l + 1)
            stores += [
                pltpu.make_async_copy(values.at[some], value_out.at[some], sems.at[0, l // 4]),
                pltpu.make_async_copy(slopes.at[some], slope_out.at[some], sems.at[1, l // 4]),
            ]
            stores[-2].start()
            stores[-1].start()
    for store in stores:
        store.wait()


VMEM = pl.BlockSpec(memory_space=pltpu.VMEM)
SMEM = pl.BlockSpec(memory_space=pltpu.SMEM)


def dev_shift(div, step):
    return [(i, i - (i // div) % 4 * div + ((i // div) % 4 + step) % 4 * div) for i in range(64)]


def local(points, charges, basis, leaf_transfer, dev_skeleton, dev_transfer, group_skeleton, neighbours, counts, far_list):
    leaves, width = neighbours.shape
    size = lax.axis_size(AXES)
    forward = [(i, i + 1) for i in range(size - 1)]
    anywhere = pl.BlockSpec(memory_space=pl.ANY)
    light = pl.CostEstimate(flops=1000, bytes_accessed=1000, transcendentals=0)

    def call(kernel, outs, ins, scratch, args, limit, specs=None):
        return pl.pallas_call(
            kernel,
            out_shape=tuple(jax.ShapeDtypeStruct(shape, kind) for shape, kind in outs),
            in_specs=ins,
            out_specs=tuple(specs or [SMEM if kind == jnp.int32 else VMEM for _, kind in outs]),
            scratch_shapes=scratch,
            compiler_params=pltpu.CompilerParams(vmem_limit_bytes=limit * MIB),
            cost_estimate=light,
        )(*args)

    def gathered(block, div, earlier, shifts):
        rows = 4 * block.shape[0] - 48
        came = [block] + [lax.ppermute(block, "dev", dev_shift(div, k)) for k in shifts]
        merge = lambda *refs: merge_kernel(shifts, *refs)
        return call(merge, [((rows, 128), F32)], [VMEM] * 4 + [anywhere], [], (*came, earlier), 8)[0]

    points = jnp.transpose(points, (1, 0, 2))
    skeleton = jnp.transpose(dev_skeleton, (1, 0, 2))
    total = leaves + 2 * REACH
    strip = ((REACH * 32 + 48, 256), F32)
    rows = pltpu.VMEM((leaves * 64, 128), F32)
    held = (points, charges.reshape(leaves * 32, 256), neighbours, counts, basis, leaf_transfer, dev_transfer[0], skeleton)
    wide = ((leaves, 128, 256), BF)
    pairs = ((256,), jnp.int32)
    up, down, packed, product, order, mine = call(
        lambda *refs: prepare_kernel(REACH, *refs),
        [strip, strip, wide, wide, pairs, ((40, 128), F32)],
        [pl.BlockSpec(memory_space=pltpu.HBM)] * 8,
        [rows, pltpu.VMEM((2, 48, 256), F32), pltpu.VMEM(*wide), pltpu.VMEM(*wide)]
        + [(pltpu.SMEM if h.dtype == jnp.int32 else pltpu.VMEM)(h.shape, h.dtype) for h in held]
        + [pltpu.SMEM(*pairs), pltpu.SemaphoreType.DMA((8,)), pltpu.SemaphoreType.DMA((7,))],
        held, 60, [anywhere] * 5 + [VMEM],
    )
    before = lax.ppermute(up, AXES, forward)
    after = lax.ppermute(down, AXES, [(j, i) for i, j in forward])
    partial = ((leaves, 128, 256), F32)
    slots = [pltpu.VMEM((256, 256), F32)] * DEPTH + [pltpu.VMEM((2, 256, 256), BF)] * DEPTH
    slots += [pltpu.VMEM((2, 256, 256), F8)] * DEPTH
    sources = [((leaves, 256, 32), BF), ((leaves, 64, 256), BF), ((leaves, 32, 256), F8)]
    listing = [pltpu.SMEM(*pairs), pltpu.SemaphoreType.DMA(())]
    (near0,) = call(
        lambda *refs: own_kernel(CUTS[0], *refs),
        [partial], [VMEM, anywhere], [pltpu.VMEM(*source) for source in sources] + slots, (packed, mine), 24,
    )
    mine = gathered(mine, 16, near0, (3, 2, 1))
    near1, *held = call(
        lambda *refs: first_kernel(CUTS[0], CUTS[1], *refs),
        [partial] + [((total + 1, *shape[1:]), kind) for shape, kind in sources],
        [anywhere] + [VMEM] * 4 + [anywhere], [rows] + listing + slots,
        (order, packed, before, after, near0, mine), 24,
    )
    mine = gathered(mine, 4, near1, (3, 2, 1))
    (near2,) = call(
        lambda *refs: next_kernel(CUTS[1], CUTS[2], *refs),
        [partial], [anywhere] + [VMEM] * 5 + [anywhere], listing + slots, (order, *held, packed, near1, mine), 24,
    )
    mine = gathered(mine, 1, near2, (2, 1, 3))
    theirs = lax.ppermute(mine, "group", [(0, 1), (1, 0)])
    (near3,) = call(
        lambda *refs: next_kernel(CUTS[2], leaves * width // DEPTH, *refs),
        [partial], [anywhere] + [VMEM] * 5 + [anywhere], listing + slots, (order, *held, packed, near2, mine), 24,
    )
    out = ((leaves, 32, 256), F32)
    return call(
        far_kernel, [out, out], [anywhere] + [VMEM] * 7,
        [pltpu.VMEM((32, 1024), F32), pltpu.VMEM((1024, 128), F32), pltpu.VMEM(*out), pltpu.VMEM(*out),
         pltpu.SMEM(far_list.shape, jnp.int32), pltpu.SemaphoreType.DMA(()), pltpu.SemaphoreType.DMA((2, leaves // 4))],
        (far_list, mine, theirs, skeleton, jnp.transpose(group_skeleton, (1, 0, 2)), dev_transfer[0],
         product, near3), 24, [anywhere] * 2,
    )


def solution(mesh):
    leaf = P(AXES, None, None)
    placed = (leaf, leaf, leaf, leaf, leaf, leaf, P(), P(AXES, None), P(AXES), P(AXES, None))
    return jax.shard_map(local, mesh=mesh, in_specs=placed, out_specs=(leaf, leaf), check_vma=False)
```

```python
import math

import jax
import jax.numpy as jnp
from jax import lax
from jax.experimental import pallas as pl
from jax.experimental.pallas import tpu as pltpu
from jax.sharding import PartitionSpec as P

BF = jnp.bfloat16
F32 = jnp.float32
HIGH = lax.Precision.HIGHEST
REACH = 14
NUGGET = 0.01
LENGTH = 0.8
LOG2E = math.log2(math.e)
LN2 = math.log(2.0)
ALPHA = math.sqrt(3.0) / LENGTH * LOG2E
X0 = ALPHA * ALPHA * NUGGET
VALUE_SCALE = LN2
SLOPE_SCALE = LN2 * LN2 / LENGTH
NODE_ROWS = 24
LIFT = 6
CHARGE_LIFT = 14
F8 = jnp.float8_e5m2
DEPTH = 8
CUTS = (2, 6, 12)
MIB = 2**20
AXES = ("group", "dev")


def my_rank():
    return lax.axis_index("group") * 64 + lax.axis_index("dev")


def dot(a, b):
    return jnp.dot(a, b, preferred_element_type=F32)


def dot32(a, b):
    return jnp.dot(a, b, preferred_element_type=F32, precision=HIGH)


def split2(x):
    hi = x.astype(BF)
    return hi, (x - hi.astype(F32)).astype(BF)


def split3(x):
    one = x.astype(BF).astype(F32)
    rest = x - one
    two = rest.astype(BF).astype(F32)
    return one, two, rest - two


def matern_terms(x, lift=0):
    t = x * lax.rsqrt(x)
    e = jnp.exp2(lift - t)
    return (t + LOG2E) * e, x * e


def write_parts(rows, points):
    leaves = points[0].shape[0]
    spread = rows.shape[0] // 2
    scaled = [p * ALPHA for p in points]
    square = scaled[0] * scaled[0] + scaled[1] * scaled[1] + scaled[2] * scaled[2]
    coords = [split3(value) for value in scaled]
    parts = [coords[c][part] for part in range(3) for c in range(3)]
    parts += [*split3(square + X0), *split3(square), jnp.ones_like(square)]
    for row, value in enumerate(parts):
        for h in range(2):
            rows[pl.ds(h * spread + row, leaves, stride=16), :] = value[:, 128 * h : 128 * h + 128]


def leaf_parts(rows, l):
    spread = rows.shape[0] // 2
    return jnp.concatenate([rows[pl.ds(h * spread + 16 * l, 16), :] for h in range(2)], axis=1).astype(BF)


def choice():
    row = lax.broadcasted_iota(jnp.int32, (64, 16), 0)
    column = lax.broadcasted_iota(jnp.int32, (64, 16), 1)
    source, r = row < 32, row & 31
    e = r & 7
    first = jnp.where((e == 1) | (e == 3) | (e == 7), 1, jnp.where((e == 4) | (e == 6), 2, 0))
    second = jnp.where((e == 2) | (e == 3) | (e == 6), 1, jnp.where((e == 5) | (e == 7), 2, 0))
    coordinate = jnp.where(source, first, second) * 3 + (r >> 3)
    early, late = jnp.where(source, 15, r - 15), jnp.where(source, r - 15, 15)
    wanted = jnp.where(r < 24, coordinate, jnp.where(r < 27, early, jnp.where(r < 30, late, -1)))
    scale = jnp.where(source & (r < 24), -2.0, 1.0)
    return jnp.where(column == wanted, scale, 0.0).astype(BF)


def dot_t(a, b):
    return lax.dot_general(a, b, (((1,), (1,)), ((), ())), preferred_element_type=F32)


def node_block(packed, basis, leaf_transfer, dev_transfer, skeleton, product, out, meanwhile):
    high, low = jnp.zeros((64, 64), F32), jnp.zeros((32, 64), F32)
    for l in range(basis.shape[0]):
        left, left_low = split2(leaf_transfer[l])
        right, right_low = split2(basis[l])
        both = dot(jnp.concatenate([left, left_low], axis=0), right)
        one, two = split2(both[:64] + both[64:] + dot(left, right_low))
        product[l, 0:64, :], product[l, 64:128, :] = one, two
        high += dot_t(packed[l, 64:128, :], one)
        low += dot_t(packed[l, 64:96, :], two)
    meanwhile()
    total = high[:32] + high[32:] + low
    image = lax.dot_general(
        total, dev_transfer[...], (((1,), (1,)), ((), ())), precision=HIGH, preferred_element_type=F32
    )
    out[0:16, :] = jnp.concatenate([total[:16], total[16:]], axis=1)
    out[16:24, :] = jnp.zeros((8, 128), F32)
    for c in range(3):
        out[16 + c : 17 + c, 0:64] = skeleton[c]
    out[24:40, :] = jnp.concatenate([image[:16], image[16:]], axis=1)


def prepare_kernel(reach, points_in, charges_in, neighbours_in, counts_in, basis_in, leaf_transfer_in, dev_transfer_in,
                   skeleton_in, up, down, packed_out, product_out, order_out, block,
                   rows, edges, packed, product, points, charges, neighbours, counts, basis, leaf_transfer, dev_transfer,
                   skeleton, order, load_sems, store_sems):
    leaves, width = neighbours.shape
    sources = (points_in, charges_in, neighbours_in, counts_in, basis_in, leaf_transfer_in, dev_transfer_in, skeleton_in)
    targets = (points, charges, neighbours, counts, basis, leaf_transfer, dev_transfer, skeleton)
    loads = [pltpu.make_async_copy(a, b, load_sems.at[i]) for i, (a, b) in enumerate(zip(sources, targets))]
    for load in loads:
        load.start()
    stores = []

    def store(source, target):
        stores.append(pltpu.make_async_copy(source, target, store_sems.at[len(stores)]))
        stores[-1].start()

    moved = 32 * reach
    loads[0].wait()
    coords = [points[c] for c in range(3)]
    for i, first in enumerate((leaves - reach, 0)):
        for c in range(3):
            edges[i, 16 * c : 16 * c + reach, :] = coords[c][first : first + reach]
            edges[i, 16 * c + reach : 16 * c + 16, :] = jnp.zeros((16 - reach, 256), F32)
        store(edges.at[i], (up, down)[i].at[pl.ds(moved, 48)])
    write_parts(rows, coords)
    chosen = choice()
    for l in range(leaves):
        packed[l, 0:64, :] = dot(chosen, leaf_parts(rows, l)).astype(BF)
    loads[1].wait()
    store(charges.at[pl.ds(32 * (leaves - reach), moved)], up.at[pl.ds(0, moved)])
    store(charges.at[pl.ds(0, moved)], down.at[pl.ds(0, moved)])
    for l in range(leaves):
        packed[l, 64:96, :], packed[l, 96:128, :] = split2(charges[32 * l : 32 * l + 32, :])
    store(packed, packed_out)
    for load in loads[4:]:
        load.wait()

    def listing():
        store(product, product_out)
        loads[2].wait()
        loads[3].wait()
        base = my_rank() * leaves - reach

        def note(slot, at):
            for leaf in range(leaves):
                chosen = jnp.clip(neighbours[leaf, slot] - base, 0, leaves + 2 * reach - 1)
                order[at] = leaf * 64 + chosen
                at = at + (slot < counts[leaf]).astype(jnp.int32)
            return at

        ends = lax.fori_loop(0, width, note, 0)
        for k in range(DEPTH):
            order[ends + k] = leaves + 2 * reach
        order[order.shape[0] - 1] = (ends + DEPTH - 1) // DEPTH
        store(order, order_out)

    node_block(packed, basis, leaf_transfer, dev_transfer, skeleton, product, block, listing)
    for one in stores:
        one.wait()


def merge_kernel(shifts, own, one, two, three, earlier, out):
    del earlier
    count = one.shape[0] - 16
    for i, ref in zip((0, *shifts), (own, one, two, three)):
        out[count * i : count * i + count, :] = ref[:count, :]
    out[4 * count :, :] = (own[count:, :] + one[count:, :]) + (two[count:, :] + three[count:, :])


def near_pairs(lo, hi, order, wa, c2, c8, ua, start, acc, slots, load=None):
    xs, highs, lows = slots[:DEPTH], slots[DEPTH : 2 * DEPTH], slots[2 * DEPTH :]

    def begin(l, carry):
        acc[l] = jnp.zeros(acc.shape[1:], F32) if start is None else start[l]
        return carry

    lax.fori_loop(0, acc.shape[0], begin, 0)
    highs[DEPTH - 1][...] = jnp.zeros(highs[0].shape, BF)
    lows[DEPTH - 1][...] = jnp.zeros(lows[0].shape, F8)
    if load is not None:
        load.wait()
        last = order[order.shape[0] - 1]
        lo, hi = jnp.minimum(lo, last), jnp.minimum(hi, last)

    def distances(i):
        pair = order[i]
        return dot(wa[pair % 64], ua[pair // 64])

    def gather_up(i, b):
        pair = order[i]
        c, small, target = c2[pair % 64], c8[pair % 64], pair // 64
        one, two = dot(c, highs[b][0]), dot(small, lows[b][0]) * 2.0**-CHARGE_LIFT
        three, four = dot(c, highs[b][1]), dot(small, lows[b][1]) * 2.0**-CHARGE_LIFT
        acc[target, 0:32, :] += one[:32] + two
        acc[target, 32:64, :] += one[32:]
        acc[target, 64:96, :] += three[:32] + four
        acc[target, 96:128, :] += three[32:]

    def step(i, b):
        xs[(b + 1) % DEPTH][...] = distances(jnp.minimum(i + 1, DEPTH * hi - 1))
        for k, term in enumerate(matern_terms(xs[b][...], LIFT)):
            high = term.astype(BF)
            highs[b][k] = high
            lows[b][k] = (term - high.astype(F32)).astype(F8)
        gather_up(jnp.maximum(i - 1, DEPTH * lo), (b - 1) % DEPTH)

    def body(j, carry):
        for u in range(DEPTH):
            step(j * DEPTH + u, u)
        return carry

    @pl.when(jnp.asarray(hi > lo))
    def _():
        xs[0][...] = distances(DEPTH * lo)
        lax.fori_loop(lo, hi, body, 0)
        gather_up(DEPTH * hi - 1, DEPTH - 1)


def small_charges(high):
    return (high.astype(F32) * 2.0**CHARGE_LIFT).astype(F8)


def unpack(packed, wa, c2, c8, offset):
    for l in range(packed.shape[0]):
        wa[offset + l] = jnp.transpose(packed[l, 0:32, :].astype(F32)).astype(BF)
        c2[offset + l] = packed[l, 64:128, :]
        c8[offset + l] = small_charges(packed[l, 64:96, :])


class Targets:
    def __init__(self, packed):
        self.packed = packed

    def __getitem__(self, i):
        return self.packed[i, 32:64, :]


class Selves:
    def __getitem__(self, i):
        return i * 65


def own_kernel(end, packed, earlier, acc, wa, c2, c8, *slots):
    del earlier
    unpack(packed, wa, c2, c8, 0)
    near_pairs(0, end, Selves(), wa, c2, c8, Targets(packed), None, acc, slots)


def first_kernel(begin, end, order_in, packed, before, after, start, earlier, acc, wa, c2, c8, rows, order, sem, *slots):
    del earlier
    load = pltpu.make_async_copy(order_in, order, sem)
    load.start()
    leaves, half = packed.shape[0], before.shape[0] // 35
    total = leaves + 2 * half
    unpack(packed, wa, c2, c8, half)
    chosen = choice()[:32]
    for ref, offset in ((before, 0), (after, half + leaves)):
        write_parts(rows, [ref[32 * half + 16 * c : 32 * half + 16 * c + half, :] for c in range(3)])
        for l in range(half):
            wa[offset + l] = jnp.transpose(dot(chosen, leaf_parts(rows, l))).astype(BF)
            high, low = split2(ref[32 * l : 32 * l + 32, :])
            c2[offset + l, 0:32, :], c2[offset + l, 32:64, :] = high, low
            c8[offset + l] = small_charges(high)
    wa[total] = wa[half]
    c2[total] = jnp.zeros(c2.shape[1:], BF)
    c8[total] = jnp.zeros(c8.shape[1:], F8)
    near_pairs(begin, end, order, wa, c2, c8, Targets(packed), start, acc, slots, load)


def next_kernel(begin, end, order_in, wa, c2, c8, packed, start, earlier, acc, order, sem, *slots):
    del earlier
    load = pltpu.make_async_copy(order_in, order, sem)
    load.start()
    near_pairs(begin, end, order, wa, c2, c8, Targets(packed), start, acc, slots, load)


def far_kernel(far_list_in, mine, theirs, own_skeleton, groups, dev_transfer, product, near, value_out, slope_out,
               coefs, kernels, values, slopes, far_list, load_sem, sems):
    load = pltpu.make_async_copy(far_list_in, far_list, load_sem)
    load.start()
    leaves = product.shape[0]
    group, node = lax.axis_index("group"), lax.axis_index("dev")

    def pair_kernel(column, row):
        x = jnp.full((64, 64), X0, F32)
        for c in range(3):
            d = (column[:, c : c + 1] - row[c : c + 1, :]) * ALPHA
            x = x + d * d
        value, slope = matern_terms(x)
        return jnp.concatenate([value * VALUE_SCALE, slope * SLOPE_SCALE], axis=1)

    other = theirs[theirs.shape[0] - 16 :, :]
    other = jnp.concatenate([other[:, :64], other[:, 64:]], axis=0)
    near_group, far_group = groups[:, pl.ds(group, 1), :][:, 0], groups[:, pl.ds(1 - group, 1), :][:, 0]
    column = jnp.transpose(jnp.concatenate([far_group, jnp.zeros((5, 64), F32)], axis=0))
    top = dot32(other, pair_kernel(column, near_group))
    top = jnp.concatenate([top[:, :64], top[:, 64:]], axis=0)
    top = dot32(top, dev_transfer[...])
    load.wait()
    own = jnp.concatenate([own_skeleton[c] for c in range(3)], axis=0)
    for j in range(far_list.shape[1]):
        s = far_list[0, j]
        x, z, y = node - s, node // 4 - s % 64 // 4, node // 16 - s % 64 // 16
        row = pl.multiple_of(((x & 3) * 16 + (z & 3) * 4 + (y & 3)) * NODE_ROWS, 8)
        block = jnp.where(s // 64 == group, mine[pl.ds(row, NODE_ROWS), :], theirs[pl.ds(row, NODE_ROWS), :])
        coefs[:, 64 * j : 64 * j + 64] = jnp.concatenate([block[:16, :64], block[:16, 64:]], axis=0)
        kernels[64 * j : 64 * j + 64, :] = pair_kernel(jnp.transpose(block[16:24, :])[:64], own)
    coef, coef_low = split2(coefs[...])
    kernel, kernel_low = split2(kernels[...])
    both = dot(jnp.concatenate([coef, coef_low], axis=0), kernel)
    far = both[:32] + both[32:] + dot(coef, kernel_low)
    far = jnp.concatenate([far[:, :64], far[:, 64:]], axis=0)
    local_dev, local_low = split2(far + top)
    local_both = jnp.concatenate([local_dev, local_low], axis=0)
    stores = []
    for l in range(leaves):
        both = dot(local_both, product[l, 0:64, :])
        part = both[:64] + both[64:] + dot(local_dev, product[l, 64:128, :])
        both = near[l]
        values[l] = (both[0:32] + both[32:64]) * (VALUE_SCALE * 2.0**-LIFT) + part[:32]
        slopes[l] = (both[64:96] + both[96:128]) * (SLOPE_SCALE * 2.0**-LIFT) + part[32:]
        if l % 4 == 3:
            some = slice(l - 3, l + 1)
            stores += [
                pltpu.make_async_copy(values.at[some], value_out.at[some], sems.at[0, l // 4]),
                pltpu.make_async_copy(slopes.at[some], slope_out.at[some], sems.at[1, l // 4]),
            ]
            stores[-2].start()
            stores[-1].start()
    for store in stores:
        store.wait()


VMEM = pl.BlockSpec(memory_space=pltpu.VMEM)
SMEM = pl.BlockSpec(memory_space=pltpu.SMEM)


def dev_shift(div, step):
    return [(i, i - (i // div) % 4 * div + ((i // div) % 4 + step) % 4 * div) for i in range(64)]


def local(points, charges, basis, leaf_transfer, dev_skeleton, dev_transfer, group_skeleton, neighbours, counts, far_list):
    leaves, width = neighbours.shape
    size = lax.axis_size(AXES)
    forward = [(i, i + 1) for i in range(size - 1)]
    anywhere = pl.BlockSpec(memory_space=pl.ANY)
    light = pl.CostEstimate(flops=1000, bytes_accessed=1000, transcendentals=0)

    def call(kernel, outs, ins, scratch, args, limit, specs=None):
        return pl.pallas_call(
            kernel,
            out_shape=tuple(jax.ShapeDtypeStruct(shape, kind) for shape, kind in outs),
            in_specs=ins,
            out_specs=tuple(specs or [SMEM if kind == jnp.int32 else VMEM for _, kind in outs]),
            scratch_shapes=scratch,
            compiler_params=pltpu.CompilerParams(vmem_limit_bytes=limit * MIB),
            cost_estimate=light,
        )(*args)

    def gathered(block, div, earlier, shifts):
        rows = 4 * block.shape[0] - 48
        came = [block] + [lax.ppermute(block, "dev", dev_shift(div, k)) for k in shifts]
        merge = lambda *refs: merge_kernel(shifts, *refs)
        return call(merge, [((rows, 128), F32)], [VMEM] * 4 + [anywhere], [], (*came, earlier), 8)[0]

    points = jnp.transpose(points, (1, 0, 2))
    skeleton = jnp.transpose(dev_skeleton, (1, 0, 2))
    total = leaves + 2 * REACH
    strip = ((REACH * 32 + 48, 256), F32)
    rows = pltpu.VMEM((leaves * 32, 128), F32)
    held = (points, charges.reshape(leaves * 32, 256), neighbours, counts, basis, leaf_transfer, dev_transfer[0], skeleton)
    wide = ((leaves, 128, 256), BF)
    pairs = ((256,), jnp.int32)
    up, down, packed, product, order, mine = call(
        lambda *refs: prepare_kernel(REACH, *refs),
        [strip, strip, wide, wide, pairs, ((40, 128), F32)],
        [pl.BlockSpec(memory_space=pltpu.HBM)] * 8,
        [rows, pltpu.VMEM((2, 48, 256), F32), pltpu.VMEM(*wide), pltpu.VMEM(*wide)]
        + [(pltpu.SMEM if h.dtype == jnp.int32 else pltpu.VMEM)(h.shape, h.dtype) for h in held]
        + [pltpu.SMEM(*pairs), pltpu.SemaphoreType.DMA((8,)), pltpu.SemaphoreType.DMA((7,))],
        held, 60, [anywhere] * 5 + [VMEM],
    )
    before = lax.ppermute(up, AXES, forward)
    after = lax.ppermute(down, AXES, [(j, i) for i, j in forward])
    partial = ((leaves, 128, 256), F32)
    slots = [pltpu.VMEM((256, 256), F32)] * DEPTH + [pltpu.VMEM((2, 256, 256), BF)] * DEPTH
    slots += [pltpu.VMEM((2, 256, 256), F8)] * DEPTH
    sources = [((leaves, 256, 32), BF), ((leaves, 64, 256), BF), ((leaves, 32, 256), F8)]
    listing = [pltpu.SMEM(*pairs), pltpu.SemaphoreType.DMA(())]
    (near0,) = call(
        lambda *refs: own_kernel(CUTS[0], *refs),
        [partial], [VMEM, anywhere], [pltpu.VMEM(*source) for source in sources] + slots, (packed, mine), 24,
    )
    mine = gathered(mine, 16, near0, (2, 3, 1))
    near1, *held = call(
        lambda *refs: first_kernel(CUTS[0], CUTS[1], *refs),
        [partial] + [((total + 1, *shape[1:]), kind) for shape, kind in sources],
        [anywhere] + [VMEM] * 4 + [anywhere], [rows] + listing + slots,
        (order, packed, before, after, near0, mine), 24,
    )
    mine = gathered(mine, 4, near1, (2, 3, 1))
    (near2,) = call(
        lambda *refs: next_kernel(CUTS[1], CUTS[2], *refs),
        [partial], [anywhere] + [VMEM] * 5 + [anywhere], listing + slots, (order, *held, packed, near1, mine), 24,
    )
    mine = gathered(mine, 1, near2, (3, 1, 2))
    theirs = lax.ppermute(mine, "group", [(0, 1), (1, 0)])
    (near3,) = call(
        lambda *refs: next_kernel(CUTS[2], leaves * width // DEPTH, *refs),
        [partial], [anywhere] + [VMEM] * 5 + [anywhere], listing + slots, (order, *held, packed, near2, mine), 24,
    )
    out = ((leaves, 32, 256), F32)
    return call(
        far_kernel, [out, out], [anywhere] + [VMEM] * 7,
        [pltpu.VMEM((32, 1024), F32), pltpu.VMEM((1024, 128), F32), pltpu.VMEM(*out), pltpu.VMEM(*out),
         pltpu.SMEM(far_list.shape, jnp.int32), pltpu.SemaphoreType.DMA(()), pltpu.SemaphoreType.DMA((2, leaves // 4))],
        (far_list, mine, theirs, skeleton, jnp.transpose(group_skeleton, (1, 0, 2)), dev_transfer[0],
         product, near3), 24, [anywhere] * 2,
    )


def solution(mesh):
    leaf = P(AXES, None, None)
    placed = (leaf, leaf, leaf, leaf, leaf, leaf, P(), P(AXES, None), P(AXES), P(AXES, None))
    return jax.shard_map(local, mesh=mesh, in_specs=placed, out_specs=(leaf, leaf), check_vma=False)
```

```python
import math

import jax
import jax.numpy as jnp
from jax import lax
from jax.experimental import pallas as pl
from jax.experimental.pallas import tpu as pltpu
from jax.sharding import PartitionSpec as P

BF = jnp.bfloat16
F32 = jnp.float32
HIGH = lax.Precision.HIGHEST
REACH = 14
NUGGET = 0.01
LENGTH = 0.8
LOG2E = math.log2(math.e)
LN2 = math.log(2.0)
ALPHA = math.sqrt(3.0) / LENGTH * LOG2E
X0 = ALPHA * ALPHA * NUGGET
VALUE_SCALE = LN2
SLOPE_SCALE = LN2 * LN2 / LENGTH
NODE_ROWS = 24
LIFT = 6
CHARGE_LIFT = 14
F8 = jnp.float8_e5m2
DEPTH = 8
CUTS = (2, 6, 12)
MIB = 2**20
AXES = ("group", "dev")


def my_rank():
    return lax.axis_index("group") * 64 + lax.axis_index("dev")


def dot(a, b):
    return jnp.dot(a, b, preferred_element_type=F32)


def dot32(a, b):
    return jnp.dot(a, b, preferred_element_type=F32, precision=HIGH)


def split2(x):
    hi = x.astype(BF)
    return hi, (x - hi.astype(F32)).astype(BF)


def split3(x):
    one = x.astype(BF).astype(F32)
    rest = x - one
    two = rest.astype(BF).astype(F32)
    return one, two, rest - two


def matern_terms(x, lift=0):
    t = x * lax.rsqrt(x)
    e = jnp.exp2(lift - t)
    return (t + LOG2E) * e, x * e


def write_parts(rows, points):
    leaves = points[0].shape[0]
    spread = rows.shape[0] // 2
    scaled = [p * ALPHA for p in points]
    square = scaled[0] * scaled[0] + scaled[1] * scaled[1] + scaled[2] * scaled[2]
    coords = [split3(value) for value in scaled]
    parts = [coords[c][part] for part in range(3) for c in range(3)]
    parts += [*split3(square + X0), *split3(square), jnp.ones_like(square)]
    for row, value in enumerate(parts):
        for h in range(2):
            rows[pl.ds(h * spread + row, leaves, stride=16), :] = value[:, 128 * h : 128 * h + 128]


def leaf_parts(rows, l):
    spread = rows.shape[0] // 2
    return jnp.concatenate([rows[pl.ds(h * spread + 16 * l, 16), :] for h in range(2)], axis=1).astype(BF)


def choice():
    row = lax.broadcasted_iota(jnp.int32, (64, 16), 0)
    column = lax.broadcasted_iota(jnp.int32, (64, 16), 1)
    source, r = row < 32, row & 31
    e = r & 7
    first = jnp.where((e == 1) | (e == 3) | (e == 7), 1, jnp.where((e == 4) | (e == 6), 2, 0))
    second = jnp.where((e == 2) | (e == 3) | (e == 6), 1, jnp.where((e == 5) | (e == 7), 2, 0))
    coordinate = jnp.where(source, first, second) * 3 + (r >> 3)
    early, late = jnp.where(source, 15, r - 15), jnp.where(source, r - 15, 15)
    wanted = jnp.where(r < 24, coordinate, jnp.where(r < 27, early, jnp.where(r < 30, late, -1)))
    scale = jnp.where(source & (r < 24), -2.0, 1.0)
    return jnp.where(column == wanted, scale, 0.0).astype(BF)


def dot_t(a, b):
    return lax.dot_general(a, b, (((1,), (1,)), ((), ())), preferred_element_type=F32)


def node_block(packed, basis, leaf_transfer, dev_transfer, skeleton, product, out, meanwhile):
    high, low = jnp.zeros((64, 64), F32), jnp.zeros((32, 64), F32)
    for l in range(basis.shape[0]):
        left, left_low = split2(leaf_transfer[l])
        right, right_low = split2(basis[l])
        both = dot(jnp.concatenate([left, left_low], axis=0), right)
        one, two = split2(both[:64] + both[64:] + dot(left, right_low))
        product[l, 0:64, :], product[l, 64:128, :] = one, two
        high += dot_t(packed[l, 64:128, :], one)
        low += dot_t(packed[l, 64:96, :], two)
    meanwhile()
    total = high[:32] + high[32:] + low
    image = lax.dot_general(
        total, dev_transfer[...], (((1,), (1,)), ((), ())), precision=HIGH, preferred_element_type=F32
    )
    out[0:16, :] = jnp.concatenate([total[:16], total[16:]], axis=1)
    out[16:24, :] = jnp.zeros((8, 128), F32)
    for c in range(3):
        out[16 + c : 17 + c, 0:64] = skeleton[c]
    out[24:40, :] = jnp.concatenate([image[:16], image[16:]], axis=1)


def prepare_kernel(reach, points_in, charges_in, neighbours_in, counts_in, basis_in, leaf_transfer_in, dev_transfer_in,
                   skeleton_in, up, down, packed_out, product_out, order_out, block,
                   rows, edges, packed, product, points, charges, neighbours, counts, basis, leaf_transfer, dev_transfer,
                   skeleton, order, load_sems, store_sems):
    leaves, width = neighbours.shape
    sources = (points_in, charges_in, neighbours_in, counts_in, basis_in, leaf_transfer_in, dev_transfer_in, skeleton_in)
    targets = (points, charges, neighbours, counts, basis, leaf_transfer, dev_transfer, skeleton)
    loads = [pltpu.make_async_copy(a, b, load_sems.at[i]) for i, (a, b) in enumerate(zip(sources, targets))]
    for load in loads:
        load.start()
    stores = []

    def store(source, target):
        stores.append(pltpu.make_async_copy(source, target, store_sems.at[len(stores)]))
        stores[-1].start()

    moved = 32 * reach
    loads[0].wait()
    coords = [points[c] for c in range(3)]
    for i, first in enumerate((leaves - reach, 0)):
        for c in range(3):
            edges[i, 16 * c : 16 * c + reach, :] = coords[c][first : first + reach]
            edges[i, 16 * c + reach : 16 * c + 16, :] = jnp.zeros((16 - reach, 256), F32)
        store(edges.at[i], (up, down)[i].at[pl.ds(moved, 48)])
    write_parts(rows, coords)
    chosen = choice()
    for l in range(leaves):
        packed[l, 0:64, :] = dot(chosen, leaf_parts(rows, l)).astype(BF)
    loads[1].wait()
    store(charges.at[pl.ds(32 * (leaves - reach), moved)], up.at[pl.ds(0, moved)])
    store(charges.at[pl.ds(0, moved)], down.at[pl.ds(0, moved)])
    for l in range(leaves):
        packed[l, 64:96, :], packed[l, 96:128, :] = split2(charges[32 * l : 32 * l + 32, :])
    store(packed, packed_out)
    for load in loads[4:]:
        load.wait()

    def listing():
        store(product, product_out)
        loads[2].wait()
        loads[3].wait()
        base = my_rank() * leaves - reach

        def note(slot, at):
            for leaf in range(leaves):
                chosen = jnp.clip(neighbours[leaf, slot] - base, 0, leaves + 2 * reach - 1)
                order[at] = leaf * 64 + chosen
                at = at + (slot < counts[leaf]).astype(jnp.int32)
            return at

        ends = lax.fori_loop(0, width, note, 0)
        for k in range(DEPTH):
            order[ends + k] = leaves + 2 * reach
        order[order.shape[0] - 1] = (ends + DEPTH - 1) // DEPTH
        store(order, order_out)

    node_block(packed, basis, leaf_transfer, dev_transfer, skeleton, product, block, listing)
    for one in stores:
        one.wait()


def merge_kernel(shifts, own, one, two, three, earlier, out):
    del earlier
    count = one.shape[0] - 16
    for i, ref in zip((0, *shifts), (own, one, two, three)):
        out[count * i : count * i + count, :] = ref[:count, :]
    out[4 * count :, :] = (own[count:, :] + one[count:, :]) + (two[count:, :] + three[count:, :])


def near_pairs(lo, hi, order, wa, c2, c8, ua, start, acc, slots, load=None):
    xs, highs, lows = slots[:DEPTH], slots[DEPTH : 2 * DEPTH], slots[2 * DEPTH :]

    def begin(l, carry):
        acc[l] = jnp.zeros(acc.shape[1:], F32) if start is None else start[l]
        return carry

    lax.fori_loop(0, acc.shape[0], begin, 0)
    highs[DEPTH - 1][...] = jnp.zeros(highs[0].shape, BF)
    lows[DEPTH - 1][...] = jnp.zeros(lows[0].shape, F8)
    if load is not None:
        load.wait()
        last = order[order.shape[0] - 1]
        lo, hi = jnp.minimum(lo, last), jnp.minimum(hi, last)

    def distances(i):
        pair = order[i]
        return dot(wa[pair % 64], ua[pair // 64])

    def gather_up(i, b):
        pair = order[i]
        c, small, target = c2[pair % 64], c8[pair % 64], pair // 64
        one, two = dot(c, highs[b][0]), dot(small, lows[b][0]) * 2.0**-CHARGE_LIFT
        three, four = dot(c, highs[b][1]), dot(small, lows[b][1]) * 2.0**-CHARGE_LIFT
        acc[target, 0:32, :] += one[:32] + two
        acc[target, 32:64, :] += one[32:]
        acc[target, 64:96, :] += three[:32] + four
        acc[target, 96:128, :] += three[32:]

    def step(i, b):
        xs[(b + 1) % DEPTH][...] = distances(jnp.minimum(i + 1, DEPTH * hi - 1))
        for r in range(0, 256, 32):
            for k, term in enumerate(matern_terms(xs[b][r : r + 32, :], LIFT)):
                high = term.astype(BF)
                highs[b][k, r : r + 32, :] = high
                lows[b][k, r : r + 32, :] = (term - high.astype(F32)).astype(F8)
        gather_up(jnp.maximum(i - 1, DEPTH * lo), (b - 1) % DEPTH)

    def body(j, carry):
        for u in range(DEPTH):
            step(j * DEPTH + u, u)
        return carry

    @pl.when(jnp.asarray(hi > lo))
    def _():
        xs[0][...] = distances(DEPTH * lo)
        lax.fori_loop(lo, hi, body, 0)
        gather_up(DEPTH * hi - 1, DEPTH - 1)


def small_charges(high):
    return (high.astype(F32) * 2.0**CHARGE_LIFT).astype(F8)


def unpack(packed, wa, c2, c8, offset):
    for l in range(packed.shape[0]):
        wa[offset + l] = jnp.transpose(packed[l, 0:32, :].astype(F32)).astype(BF)
        c2[offset + l] = packed[l, 64:128, :]
        c8[offset + l] = small_charges(packed[l, 64:96, :])


class Targets:
    def __init__(self, packed):
        self.packed = packed

    def __getitem__(self, i):
        return self.packed[i, 32:64, :]


class Selves:
    def __getitem__(self, i):
        return i * 65


def own_kernel(end, packed, earlier, acc, wa, c2, c8, *slots):
    del earlier
    unpack(packed, wa, c2, c8, 0)
    near_pairs(0, end, Selves(), wa, c2, c8, Targets(packed), None, acc, slots)


def first_kernel(begin, end, order_in, packed, before, after, start, earlier, acc, wa, c2, c8, rows, order, sem, *slots):
    del earlier
    load = pltpu.make_async_copy(order_in, order, sem)
    load.start()
    leaves, half = packed.shape[0], before.shape[0] // 35
    total = leaves + 2 * half
    unpack(packed, wa, c2, c8, half)
    chosen = choice()[:32]
    for ref, offset in ((before, 0), (after, half + leaves)):
        write_parts(rows, [ref[32 * half + 16 * c : 32 * half + 16 * c + half, :] for c in range(3)])
        for l in range(half):
            wa[offset + l] = jnp.transpose(dot(chosen, leaf_parts(rows, l))).astype(BF)
            high, low = split2(ref[32 * l : 32 * l + 32, :])
            c2[offset + l, 0:32, :], c2[offset + l, 32:64, :] = high, low
            c8[offset + l] = small_charges(high)
    wa[total] = wa[half]
    c2[total] = jnp.zeros(c2.shape[1:], BF)
    c8[total] = jnp.zeros(c8.shape[1:], F8)
    near_pairs(begin, end, order, wa, c2, c8, Targets(packed), start, acc, slots, load)


def next_kernel(begin, end, order_in, wa, c2, c8, packed, start, earlier, acc, order, sem, *slots):
    del earlier
    load = pltpu.make_async_copy(order_in, order, sem)
    load.start()
    near_pairs(begin, end, order, wa, c2, c8, Targets(packed), start, acc, slots, load)


def far_kernel(far_list_in, mine, theirs, own_skeleton, groups, dev_transfer, product, near, value_out, slope_out,
               coefs, kernels, values, slopes, far_list, load_sem, sems):
    load = pltpu.make_async_copy(far_list_in, far_list, load_sem)
    load.start()
    leaves = product.shape[0]
    group, node = lax.axis_index("group"), lax.axis_index("dev")

    def pair_kernel(column, row):
        x = jnp.full((64, 64), X0, F32)
        for c in range(3):
            d = (column[:, c : c + 1] - row[c : c + 1, :]) * ALPHA
            x = x + d * d
        value, slope = matern_terms(x)
        return jnp.concatenate([value * VALUE_SCALE, slope * SLOPE_SCALE], axis=1)

    other = theirs[theirs.shape[0] - 16 :, :]
    other = jnp.concatenate([other[:, :64], other[:, 64:]], axis=0)
    near_group, far_group = groups[:, pl.ds(group, 1), :][:, 0], groups[:, pl.ds(1 - group, 1), :][:, 0]
    column = jnp.transpose(jnp.concatenate([far_group, jnp.zeros((5, 64), F32)], axis=0))
    top = dot32(other, pair_kernel(column, near_group))
    top = jnp.concatenate([top[:, :64], top[:, 64:]], axis=0)
    top = dot32(top, dev_transfer[...])
    load.wait()
    own = jnp.concatenate([own_skeleton[c] for c in range(3)], axis=0)
    for j in range(far_list.shape[1]):
        s = far_list[0, j]
        x, z, y = node - s, node // 4 - s % 64 // 4, node // 16 - s % 64 // 16
        row = pl.multiple_of(((x & 3) * 16 + (z & 3) * 4 + (y & 3)) * NODE_ROWS, 8)
        block = jnp.where(s // 64 == group, mine[pl.ds(row, NODE_ROWS), :], theirs[pl.ds(row, NODE_ROWS), :])
        coefs[:, 64 * j : 64 * j + 64] = jnp.concatenate([block[:16, :64], block[:16, 64:]], axis=0)
        kernels[64 * j : 64 * j + 64, :] = pair_kernel(jnp.transpose(block[16:24, :])[:64], own)
    coef, coef_low = split2(coefs[...])
    kernel, kernel_low = split2(kernels[...])
    both = dot(jnp.concatenate([coef, coef_low], axis=0), kernel)
    far = both[:32] + both[32:] + dot(coef, kernel_low)
    far = jnp.concatenate([far[:, :64], far[:, 64:]], axis=0)
    local_dev, local_low = split2(far + top)
    local_both = jnp.concatenate([local_dev, local_low], axis=0)
    stores = []
    for l in range(leaves):
        both = dot(local_both, product[l, 0:64, :])
        part = both[:64] + both[64:] + dot(local_dev, product[l, 64:128, :])
        both = near[l]
        values[l] = (both[0:32] + both[32:64]) * (VALUE_SCALE * 2.0**-LIFT) + part[:32]
        slopes[l] = (both[64:96] + both[96:128]) * (SLOPE_SCALE * 2.0**-LIFT) + part[32:]
        if l % 4 == 3:
            some = slice(l - 3, l + 1)
            stores += [
                pltpu.make_async_copy(values.at[some], value_out.at[some], sems.at[0, l // 4]),
                pltpu.make_async_copy(slopes.at[some], slope_out.at[some], sems.at[1, l // 4]),
            ]
            stores[-2].start()
            stores[-1].start()
    for store in stores:
        store.wait()


VMEM = pl.BlockSpec(memory_space=pltpu.VMEM)
SMEM = pl.BlockSpec(memory_space=pltpu.SMEM)


def dev_shift(div, step):
    return [(i, i - (i // div) % 4 * div + ((i // div) % 4 + step) % 4 * div) for i in range(64)]


def local(points, charges, basis, leaf_transfer, dev_skeleton, dev_transfer, group_skeleton, neighbours, counts, far_list):
    leaves, width = neighbours.shape
    size = lax.axis_size(AXES)
    forward = [(i, i + 1) for i in range(size - 1)]
    anywhere = pl.BlockSpec(memory_space=pl.ANY)
    light = pl.CostEstimate(flops=1000, bytes_accessed=1000, transcendentals=0)

    def call(kernel, outs, ins, scratch, args, limit, specs=None):
        return pl.pallas_call(
            kernel,
            out_shape=tuple(jax.ShapeDtypeStruct(shape, kind) for shape, kind in outs),
            in_specs=ins,
            out_specs=tuple(specs or [SMEM if kind == jnp.int32 else VMEM for _, kind in outs]),
            scratch_shapes=scratch,
            compiler_params=pltpu.CompilerParams(vmem_limit_bytes=limit * MIB),
            cost_estimate=light,
        )(*args)

    def gathered(block, div, earlier, shifts):
        rows = 4 * block.shape[0] - 48
        came = [block] + [lax.ppermute(block, "dev", dev_shift(div, k)) for k in shifts]
        merge = lambda *refs: merge_kernel(shifts, *refs)
        return call(merge, [((rows, 128), F32)], [VMEM] * 4 + [anywhere], [], (*came, earlier), 8)[0]

    points = jnp.transpose(points, (1, 0, 2))
    skeleton = jnp.transpose(dev_skeleton, (1, 0, 2))
    total = leaves + 2 * REACH
    strip = ((REACH * 32 + 48, 256), F32)
    rows = pltpu.VMEM((leaves * 32, 128), F32)
    held = (points, charges.reshape(leaves * 32, 256), neighbours, counts, basis, leaf_transfer, dev_transfer[0], skeleton)
    wide = ((leaves, 128, 256), BF)
    pairs = ((256,), jnp.int32)
    up, down, packed, product, order, mine = call(
        lambda *refs: prepare_kernel(REACH, *refs),
        [strip, strip, wide, wide, pairs, ((40, 128), F32)],
        [pl.BlockSpec(memory_space=pltpu.HBM)] * 8,
        [rows, pltpu.VMEM((2, 48, 256), F32), pltpu.VMEM(*wide), pltpu.VMEM(*wide)]
        + [(pltpu.SMEM if h.dtype == jnp.int32 else pltpu.VMEM)(h.shape, h.dtype) for h in held]
        + [pltpu.SMEM(*pairs), pltpu.SemaphoreType.DMA((8,)), pltpu.SemaphoreType.DMA((7,))],
        held, 60, [anywhere] * 5 + [VMEM],
    )
    before = lax.ppermute(up, AXES, forward)
    after = lax.ppermute(down, AXES, [(j, i) for i, j in forward])
    partial = ((leaves, 128, 256), F32)
    slots = [pltpu.VMEM((256, 256), F32)] * DEPTH + [pltpu.VMEM((2, 256, 256), BF)] * DEPTH
    slots += [pltpu.VMEM((2, 256, 256), F8)] * DEPTH
    sources = [((leaves, 256, 32), BF), ((leaves, 64, 256), BF), ((leaves, 32, 256), F8)]
    listing = [pltpu.SMEM(*pairs), pltpu.SemaphoreType.DMA(())]
    (near0,) = call(
        lambda *refs: own_kernel(CUTS[0], *refs),
        [partial], [VMEM, anywhere], [pltpu.VMEM(*source) for source in sources] + slots, (packed, mine), 24,
    )
    mine = gathered(mine, 16, near0, (2, 3, 1))
    near1, *held = call(
        lambda *refs: first_kernel(CUTS[0], CUTS[1], *refs),
        [partial] + [((total + 1, *shape[1:]), kind) for shape, kind in sources],
        [anywhere] + [VMEM] * 4 + [anywhere], [rows] + listing + slots,
        (order, packed, before, after, near0, mine), 24,
    )
    mine = gathered(mine, 4, near1, (2, 3, 1))
    (near2,) = call(
        lambda *refs: next_kernel(CUTS[1], CUTS[2], *refs),
        [partial], [anywhere] + [VMEM] * 5 + [anywhere], listing + slots, (order, *held, packed, near1, mine), 24,
    )
    mine = gathered(mine, 1, near2, (3, 1, 2))
    theirs = lax.ppermute(mine, "group", [(0, 1), (1, 0)])
    (near3,) = call(
        lambda *refs: next_kernel(CUTS[2], leaves * width // DEPTH, *refs),
        [partial], [anywhere] + [VMEM] * 5 + [anywhere], listing + slots, (order, *held, packed, near2, mine), 24,
    )
    out = ((leaves, 32, 256), F32)
    return call(
        far_kernel, [out, out], [anywhere] + [VMEM] * 7,
        [pltpu.VMEM((32, 1024), F32), pltpu.VMEM((1024, 128), F32), pltpu.VMEM(*out), pltpu.VMEM(*out),
         pltpu.SMEM(far_list.shape, jnp.int32), pltpu.SemaphoreType.DMA(()), pltpu.SemaphoreType.DMA((2, leaves // 4))],
        (far_list, mine, theirs, skeleton, jnp.transpose(group_skeleton, (1, 0, 2)), dev_transfer[0],
         product, near3), 24, [anywhere] * 2,
    )


def solution(mesh):
    leaf = P(AXES, None, None)
    placed = (leaf, leaf, leaf, leaf, leaf, leaf, P(), P(AXES, None), P(AXES), P(AXES, None))
    return jax.shard_map(local, mesh=mesh, in_specs=placed, out_specs=(leaf, leaf), check_vma=False)
```
